512 devices in a mesh: blk: 32 (over z, x_hi), grp: 16 (over y, x_lo, core).
Axes of the slice: x: 4 (x_hi: 2, x_lo: 2; x = x_hi * 2 + x_lo), y: 4, z: 16, core: 2. Of those that a mesh axis runs over, the one named last changes fastest.
Arguments:
- images: float32 [65536, 1152], P(('blk', 'grp')), may hold values from -6 to 6
- texts: float32 [65536, 1152], P(('blk', 'grp')), may hold values from -6 to 6
- log_scale: float32 [1], replicated, may hold values from 2.3 to 3.4
- bias: float32 [1], replicated, may hold values from -3 to -1
Outputs:
- row_loss: float32 [65536], P(('blk', 'grp'))
- image_grad: float32 [65536, 1152], P(('blk', 'grp'))
- text_grad: float32 [65536, 1152], P(('blk', 'grp'))
The draws below stay inside these ranges and needn't reach their ends.
All inputs are finite; a program needn't handle non-finite values.
Results may differ from the reference program's by a relative error of at most 0.0056.
Values may be sent and summed in bfloat16 or wider, within the bound.
A program may use at most 64 MiB of HBM per device.

```python
import jax
import jax.numpy as jnp
from jax import lax

D = 1152
STEPS = 2
BLOCK = 2048
BATCH = 65536
N_BLK = 32


def steps_of(rng, dims, pieces, least, top_value):
    level, own = 1.0, jax.random.fold_in(rng, 6)
    for dim, blocks in pieces:
        heights = jnp.exp(jax.random.uniform(jax.random.fold_in(own, dim), (blocks,), jnp.float32, least / len(pieces), top_value / len(pieces)))
        level = level * jnp.repeat(heights, dims[dim] // blocks).reshape([-1 if axis == dim else 1 for axis in range(len(dims))])
    return level


def noise(own_key, shape, scale, limit, split=(), kind=jnp.bfloat16):
    drawn = scale * jax.random.normal(own_key, shape, jnp.float32)
    if split:
        drawn = drawn * steps_of(own_key, shape, split, -0.22, 0.18)
    return jnp.clip(drawn, -limit, limit).astype(kind)


def setup_inputs(seed: int = 0) -> dict:
    arg_keys = jax.random.split(jax.random.key(seed), 5)
    images = noise(arg_keys[0], (BATCH, D), 1.0, 6.0, ((0, 512),), jnp.float32)
    texts = noise(arg_keys[1], (BATCH, D), 1.0, 6.0, ((0, 512),), jnp.float32)
    log_scale = jnp.clip(jax.random.uniform(arg_keys[2], (1,), jnp.float32, 2.3, 3.4), 2.3, 3.4)
    bias = jnp.clip(jax.random.uniform(arg_keys[3], (1,), jnp.float32, -3.0, -1.0), -3.0, -1.0)
    return {"images": images, "texts": texts, "log_scale": log_scale, "bias": bias}


def prepare(values):
    inverse = lax.rsqrt(lax.optimization_barrier(jnp.sum(values * values, axis=1, keepdims=True)) + 1e-06)
    unit = values * inverse
    return (inverse, unit, unit.astype(jnp.bfloat16))

def score_block(left, right, temper, offset, first):
    logits = temper * jnp.dot(left, right.T, preferred_element_type=jnp.float32) + offset
    paired = jnp.eye(left.shape[0], dtype=jnp.float32) * first
    losses = jnp.where(paired > 0.5, jax.nn.softplus(-logits), jax.nn.softplus(logits))
    weights = (temper * (jax.nn.sigmoid(logits) - paired)).astype(jnp.bfloat16)
    return (lax.optimization_barrier(jnp.sum(losses, axis=1)), jnp.dot(weights, right, preferred_element_type=jnp.float32))

def backnorm(inverse, unit, grad):
    return inverse * (grad - unit * lax.optimization_barrier(jnp.sum(unit * grad, axis=1, keepdims=True)))

def reference(images, texts, log_scale, bias):
    temper = jnp.exp(log_scale[0])
    offset = bias[0]
    inv_image, image_hat, image_low = prepare(images)
    inv_text, text_hat, text_low = prepare(texts)
    image_blocks = image_low.reshape(N_BLK, BLOCK, D)
    text_blocks = text_low.reshape(N_BLK, BLOCK, D)
    loss_total = jnp.zeros((N_BLK, BLOCK), jnp.float32)
    grad_image = jnp.zeros((N_BLK, BLOCK, D), jnp.float32)
    grad_text = jnp.zeros((N_BLK, BLOCK, D), jnp.float32)
    for step in range(STEPS):
        first = 1.0 if step == 0 else 0.0
        text_seen = jnp.roll(text_blocks, step, axis=0)
        image_seen = jnp.roll(image_blocks, -step, axis=0)
        losses, gimage = lax.map(lambda pair: score_block(pair[0], pair[1], temper, offset, first), (image_blocks, text_seen))
        unused, gtext = lax.map(lambda pair: score_block(pair[0], pair[1], temper, offset, first), (text_blocks, image_seen))
        loss_total = loss_total + losses
        grad_image = grad_image + gimage
        grad_text = grad_text + gtext
    row_loss = loss_total.reshape(BATCH) / (STEPS * BLOCK)
    image_grad = backnorm(inv_image, image_hat, grad_image.reshape(BATCH, D))
    text_grad = backnorm(inv_text, text_hat, grad_text.reshape(BATCH, D))
    return (row_loss, image_grad, text_grad)
```

```python
import functools

import jax
import jax.numpy as jnp
from jax import lax
from jax.experimental import pallas as pl
from jax.experimental.pallas import tpu as pltpu
from jax.sharding import PartitionSpec as P

STEPS = 2
MESH = pl.DeviceIdType.MESH
BF = jnp.bfloat16
F32 = jnp.float32

OWN, PAIR, NEAR, FAR = 0, 1, 2, 3
Y_OFF = (0, 1, 3, 2)


def places(n_blk):
    b = lax.axis_index("blk")
    g = lax.axis_index("grp")
    core = lax.rem(g, 2)
    x_lo = lax.rem(g // 2, 2)
    y = g // 4
    nxt = lax.rem(b + 1, n_blk)
    prv = lax.rem(b + n_blk - 1, n_blk)

    def member(yy, xx, kk):
        return (yy * 2 + xx) * 2 + kk

    sibling = (b, member(y, x_lo, 1 - core))
    pair = (b, member(y, 1 - x_lo, core))
    near_to = (nxt, member(y, 1 - x_lo, core))
    far_to = (nxt, member(y, x_lo, core))
    near_of = (prv, member(y, 1 - x_lo, core))
    far_of = (prv, member(y, x_lo, core))
    ring = [(b, member(lax.rem(y + d, 4), x_lo, core)) for d in Y_OFF[1:]]
    return sibling, pair, near_to, far_to, near_of, far_of, ring


def inverse_norm(values):
    return lax.rsqrt(jnp.sum(values * values, axis=1, keepdims=True) + 1e-06)


def kernel(n_blk, mean, ls_ref, bi_ref, img_hbm, txt_hbm, loss_ref, gi_hbm, gt_hbm,
           img, txt, gi, gt, ib, tb, coef, loss, sib_out, sib_in, t_out, t_in, i_out, i_in, l_in,
           lsem, ssem, rsem):
    rows = img.shape[0]
    sibling, pair, near_to, far_to, near_of, far_of, ring = places(n_blk)
    load_t = pltpu.make_async_copy(txt_hbm, txt, lsem.at[0])
    load_i = pltpu.make_async_copy(img_hbm, img, lsem.at[1])
    load_t.start()
    load_i.start()

    barrier = pltpu.get_barrier_semaphore()
    others = [sibling, pair, near_to, far_to, near_of, far_of] + ring
    for other in others:
        pl.semaphore_signal(barrier, inc=1, device_id=other, device_id_type=MESH)

    count = iter(range(64))

    def send(src, dst, to):
        s = next(count)
        return pltpu.make_async_remote_copy(
            src_ref=src, dst_ref=dst, send_sem=ssem.at[s], recv_sem=rsem.at[s],
            device_id=to, device_id_type=MESH)

    load_t.wait()
    inv_t = inverse_norm(txt[...])
    tb[0, 0] = (txt[...] * inv_t).astype(BF)
    load_i.wait()
    inv_i = inverse_norm(img[...])
    ib[0] = (img[...] * inv_i).astype(BF)
    pl.semaphore_wait(barrier, len(others))

    t_copies = [send(tb.at[0, 0], tb.at[s, 0], to)
                for s, to in ((PAIR, pair), (NEAR, near_to), (FAR, far_to))]
    i_copies = [send(ib.at[0], ib.at[slot], ring[j]) for j, slot in ((0, 2), (1, 1), (2, 3))]
    s_copies = [send(tb.at[s, 0], tb.at[s, 1], sibling) for s in range(4)]
    for c in (t_copies[0], i_copies[0], t_copies[1], i_copies[1], t_copies[2], i_copies[2], s_copies[0]):
        c.start()

    temper = jnp.exp(jnp.full((1, rows), ls_ref[0], F32))
    offset = bi_ref[0]
    loss[...] = jnp.zeros_like(loss)

    def score(s, lo, hi):
        left = tb[s].reshape(2 * rows, tb.shape[-1])
        for slot in range(lo, hi):
            logit = lax.dot_general(left, ib[slot], (((1,), (1,)), ((), ())), preferred_element_type=F32)
            logit = temper * logit + offset
            e = jnp.exp(-jnp.abs(logit))
            r = 1.0 / (1.0 + e)
            weight = jnp.where(logit >= 0, r, e * r)
            signed = logit
            if s == OWN and slot == 0:
                paired = (lax.broadcasted_iota(jnp.int32, logit.shape, 0)
                          == lax.broadcasted_iota(jnp.int32, logit.shape, 1))
                weight = weight - paired.astype(F32)
                signed = jnp.where(paired, -logit, logit)
            lost = jnp.maximum(signed, 0.0) + jnp.where(e < 1e-3, e * (1.0 - 0.5 * e), jnp.log(1.0 + e))
            loss[slot] += jnp.sum(lost.reshape(2 * rows // 8, 8, rows), axis=0)
            coef[pl.ds(s * 2 * rows, 2 * rows), pl.ds(slot * rows, rows)] = (temper * weight).astype(BF)

    def text_partial(s):
        return jnp.dot(coef[pl.ds(s * 2 * rows, 2 * rows), :], ib[...].reshape(4 * rows, ib.shape[-1]),
                       preferred_element_type=F32)

    def image_partial(slot):
        return lax.dot_general(coef[:, pl.ds(slot * rows, rows)], tb[...].reshape(8 * rows, tb.shape[-1]),
                               (((0,), (0,)), ((), ())), preferred_element_type=F32)

    s_copies[0].wait_recv()
    score(OWN, 0, 1)
    t_copies[0].wait_recv()
    s_copies[1].start()
    t_copies[1].wait_recv()
    s_copies[2].start()
    i_copies[0].wait_recv()
    i_copies[1].wait_recv()
    score(OWN, 1, 3)
    s_copies[1].wait_recv()
    score(PAIR, 0, 3)
    s_copies[2].wait_recv()
    score(NEAR, 0, 3)
    t_copies[2].wait_recv()
    s_copies[3].start()
    i_copies[2].wait_recv()
    for s in (PAIR, NEAR, OWN):
        score(s, 3, 4)

    back = [send(sib_out.at[s], sib_in.at[s], sibling) for s in range(4)]
    t_back = [None] + [send(t_out.at[s - 1], t_in.at[s - 1], to)
                       for s, to in ((PAIR, pair), (NEAR, near_of), (FAR, far_of))]
    i_back = [None] + [send(i_out.at[j], i_in.at[(1, 0, 2)[j]], ring[j]) for j in range(3)]
    l_back = [None] + [send(loss.at[j + 1], l_in.at[(1, 0, 2)[j]], ring[j]) for j in range(3)]
    held = {}

    def start_text(s):
        part = text_partial(s)
        sib_out[s] = part[rows:].astype(BF)
        back[s].start()
        held[s] = part[:rows]

    def finish_text(s):
        back[s].wait_recv()
        whole = held[s] + sib_in[s].astype(F32)
        if s == OWN:
            gt[...] = whole
        else:
            t_out[s - 1] = whole.astype(BF)
            t_back[s].start()

    start_text(PAIR)
    start_text(NEAR)
    s_copies[3].wait_recv()
    score(FAR, 0, 4)
    finish_text(PAIR)
    finish_text(NEAR)
    start_text(FAR)
    for slot in (3, 1, 2):
        i_out[slot - 1] = image_partial(slot).astype(BF)
        i_back[slot].start()
        l_back[slot].start()
        if slot == 3:
            finish_text(FAR)
    gi[...] = image_partial(0)
    start_text(OWN)
    finish_text(OWN)

    def backnorm(values, inverse, grad):
        unit = values * inverse
        return inverse * (grad - unit * jnp.sum(unit * grad, axis=1, keepdims=True))

    for c in l_back[1:]:
        c.wait_recv()
    total = loss[0] + l_in[0] + l_in[1] + l_in[2]
    loss_ref[...] = jnp.sum(total, axis=0, keepdims=True) / mean

    for c in i_back[1:]:
        c.wait_recv()
    grad = gi[...] + i_in[0].astype(F32) + i_in[1].astype(F32) + i_in[2].astype(F32)
    gi[...] = backnorm(img[...], inv_i, grad)
    put_i = pltpu.make_async_copy(gi, gi_hbm, lsem.at[0])
    put_i.start()
    for c in t_back[1:]:
        c.wait_recv()
    grad = gt[...] + t_in[0].astype(F32) + t_in[1].astype(F32) + t_in[2].astype(F32)
    gt[...] = backnorm(txt[...], inv_t, grad)
    put_t = pltpu.make_async_copy(gt, gt_hbm, lsem.at[1])
    put_t.start()
    for c in t_copies + i_copies + s_copies + back + t_back[1:] + i_back[1:] + l_back[1:]:
        c.wait_send()
    put_i.wait()
    put_t.wait()


def body(images, texts, log_scale, bias):
    rows, width = images.shape
    n_blk = lax.axis_size("blk")
    mean = STEPS * rows * lax.axis_size("grp")
    half = functools.partial(pltpu.VMEM, dtype=BF)
    full = functools.partial(pltpu.VMEM, dtype=F32)
    any_space = pl.BlockSpec(memory_space=pl.ANY)
    row_loss, image_grad, text_grad = pl.pallas_call(
        functools.partial(kernel, n_blk, mean),
        out_shape=(
            jax.ShapeDtypeStruct((1, rows), F32),
            jax.ShapeDtypeStruct((rows, width), F32),
            jax.ShapeDtypeStruct((rows, width), F32),
        ),
        in_specs=[pl.BlockSpec(memory_space=pltpu.SMEM)] * 2 + [any_space] * 2,
        out_specs=(pl.BlockSpec(memory_space=pltpu.VMEM), any_space, any_space),
        scratch_shapes=[
            full((rows, width)), full((rows, width)), full((rows, width)), full((rows, width)),
            half((4, rows, width)),
            half((4, 2, rows, width)),
            half((8 * rows, 4 * rows)),
            full((4, 8, rows)),
            half((4, rows, width)), half((4, rows, width)),
            half((3, rows, width)), half((3, rows, width)),
            half((3, rows, width)), half((3, rows, width)),
            full((3, 8, rows)),
            pltpu.SemaphoreType.DMA((2,)),
            pltpu.SemaphoreType.DMA((23,)),
            pltpu.SemaphoreType.DMA((23,)),
        ],
        compiler_params=pltpu.CompilerParams(
            collective_id=0, has_side_effects=True, vmem_limit_bytes=40 << 20),
        name="pair_loss",
    )(log_scale, bias, images, texts)
    return row_loss.reshape(rows), image_grad, text_grad


def solution(mesh):
    in_specs = (P(("blk", "grp"), None), P(("blk", "grp"), None), P(), P())
    out_specs = (P(("blk", "grp")), P(("blk", "grp"), None), P(("blk", "grp"), None))
    return jax.shard_map(body, mesh=mesh, in_specs=in_specs, out_specs=out_specs, check_vma=False)
```

```python
import functools

import jax
import jax.numpy as jnp
from jax import lax
from jax.experimental import pallas as pl
from jax.experimental.pallas import tpu as pltpu
from jax.sharding import PartitionSpec as P

STEPS = 2
MESH = pl.DeviceIdType.MESH
BF = jnp.bfloat16
F32 = jnp.float32
N_SEMS = 36

OWN, PAIR, NEAR, FAR = 0, 1, 2, 3
RIGHT, LEFT, OPP = 1, 2, 3


def places(n_blk):
    b = lax.axis_index("blk")
    g = lax.axis_index("grp")
    core = lax.rem(g, 2)
    x_lo = lax.rem(g // 2, 2)
    y = g // 4
    nxt = lax.rem(b + 1, n_blk)
    prv = lax.rem(b + n_blk - 1, n_blk)

    def member(yy, xx, kk):
        return (yy * 2 + xx) * 2 + kk

    sibling = (b, member(y, x_lo, 1 - core))
    pair = (b, member(y, 1 - x_lo, core))
    near_to = (nxt, member(y, 1 - x_lo, core))
    near_of = (prv, member(y, 1 - x_lo, core))
    right = (b, member(lax.rem(y + 1, 4), x_lo, core))
    left = (b, member(lax.rem(y + 3, 4), x_lo, core))
    return sibling, pair, near_to, near_of, right, left


def inverse_norm(values):
    return lax.rsqrt(jnp.sum(values * values, axis=1, keepdims=True) + 1e-06)


def kernel(n_blk, mean, ls_ref, bi_ref, img_hbm, txt_hbm, loss_ref, gi_hbm, gt_hbm,
           img, txt, gi, gt, ib, tb, coef, loss, sib_out, sib_in,
           t_out, t_mid, t_in, i_out, i_mid, i_in, l_mid, l_in, lsem, ssem, rsem):
    rows, width = img.shape
    half = rows // 2
    h0, h1 = pl.ds(0, half), pl.ds(half, half)
    sibling, pair, near_to, near_of, right, left = places(n_blk)
    load_t = pltpu.make_async_copy(txt_hbm, txt, lsem.at[0])
    load_i = pltpu.make_async_copy(img_hbm, img, lsem.at[1])
    load_t.start()
    load_i.start()

    barrier = pltpu.get_barrier_semaphore()
    others = [sibling, pair, near_to, near_of, right, left]
    for other in others:
        pl.semaphore_signal(barrier, inc=1, device_id=other, device_id_type=MESH)

    sent = []

    def copy_to(src, dst, to):
        s = len(sent)
        copy = pltpu.make_async_remote_copy(
            src_ref=src, dst_ref=dst, send_sem=ssem.at[s], recv_sem=rsem.at[s],
            device_id=to, device_id_type=MESH)
        sent.append(copy)
        return copy

    def arrived(name, *copies):
        with jax.named_scope("wait_" + name):
            for c in copies:
                c.wait_recv()

    with jax.named_scope("normalize"):
        load_t.wait()
        inv_t = inverse_norm(txt[...])
        tb[OWN, 0] = (txt[...] * inv_t).astype(BF)
        load_i.wait()
        inv_i = inverse_norm(img[...])
        ib[0] = (img[...] * inv_i).astype(BF)
    with jax.named_scope("barrier"):
        pl.semaphore_wait(barrier, len(others))

    t_p0 = copy_to(tb.at[OWN, 0, h0], tb.at[PAIR, 0, h0], pair)
    t_n1 = copy_to(tb.at[OWN, 0, h1], tb.at[NEAR, 0, h1], near_to)
    i_r0 = copy_to(ib.at[0, h0], ib.at[LEFT, h0], right)
    i_l1 = copy_to(ib.at[0, h1], ib.at[RIGHT, h1], left)
    t_p1 = copy_to(tb.at[OWN, 0, h1], tb.at[PAIR, 0, h1], pair)
    t_n0 = copy_to(tb.at[OWN, 0, h0], tb.at[NEAR, 0, h0], near_to)
    i_r1 = copy_to(ib.at[0, h1], ib.at[LEFT, h1], right)
    i_l0 = copy_to(ib.at[0, h0], ib.at[RIGHT, h0], left)
    s_own = copy_to(tb.at[OWN, 0], tb.at[OWN, 1], sibling)
    for c in sent:
        c.start()
    t_f0 = copy_to(tb.at[PAIR, 0, h0], tb.at[FAR, 0, h0], near_to)
    t_f1 = copy_to(tb.at[NEAR, 0, h1], tb.at[FAR, 0, h1], pair)
    i_o0 = copy_to(ib.at[LEFT, h0], ib.at[OPP, h0], right)
    i_o1 = copy_to(ib.at[RIGHT, h1], ib.at[OPP, h1], left)
    s_pair = copy_to(tb.at[PAIR, 0], tb.at[PAIR, 1], sibling)
    s_near = copy_to(tb.at[NEAR, 0], tb.at[NEAR, 1], sibling)
    s_f0 = copy_to(tb.at[FAR, 0, h0], tb.at[FAR, 1, h0], sibling)
    s_f1 = copy_to(tb.at[FAR, 0, h1], tb.at[FAR, 1, h1], sibling)

    temper = jnp.exp(jnp.full((1, rows), ls_ref[0], F32))
    offset = bi_ref[0]
    loss[...] = jnp.zeros_like(loss)

    def score(s, lo, hi):
        with jax.named_scope(f"score_{s}_{lo}_{hi}"):
            chunk = tb[s].reshape(2 * rows, width)
            for slot in range(lo, hi):
                logit = lax.dot_general(chunk, ib[slot], (((1,), (1,)), ((), ())), preferred_element_type=F32)
                logit = temper * logit + offset
                e = jnp.exp(-jnp.abs(logit))
                v = 1.0 + e
                r = 1.0 / v
                weight = jnp.where(logit >= 0, r, e * r)
                signed = logit
                if s == OWN and slot == 0:
                    paired = (lax.broadcasted_iota(jnp.int32, logit.shape, 0)
                              == lax.broadcasted_iota(jnp.int32, logit.shape, 1))
                    weight = weight - paired.astype(F32)
                    signed = jnp.where(paired, -logit, logit)
                lost = jnp.maximum(signed, 0.0) + jnp.where(e < 1e-3, e * (1.0 - 0.5 * e), jnp.log(v))
                loss[slot] += jnp.sum(lost.reshape(2 * rows // 8, 8, rows), axis=0)
                coef[pl.ds(s * 2 * rows, 2 * rows), pl.ds(slot * rows, rows)] = (temper * weight).astype(BF)

    def image_partial(slot):
        return lax.dot_general(coef[:, pl.ds(slot * rows, rows)], tb[...].reshape(8 * rows, width),
                               (((0,), (0,)), ((), ())), preferred_element_type=F32)

    arrived("own_sibling", s_own)
    score(OWN, 0, 1)
    arrived("first_t", t_p0, t_n1)
    t_f0.start()
    t_f1.start()
    arrived("first_i", i_r0, i_l1)
    i_o0.start()
    i_o1.start()
    arrived("second_p", t_p1)
    s_pair.start()
    arrived("second_n", t_n0)
    s_near.start()
    arrived("second_i", i_r1, i_l0)
    score(OWN, 1, 3)
    arrived("pair_sibling", s_pair)
    score(PAIR, 0, 3)
    arrived("near_sibling", s_near)
    score(NEAR, 0, 3)
    arrived("far_t0", t_f0)
    s_f0.start()
    arrived("far_t1", t_f1)
    s_f1.start()
    arrived("opp_i", i_o0, i_o1)
    for s in (PAIR, NEAR, OWN):
        score(s, OPP, OPP + 1)
    arrived("far_sibling", s_f0, s_f1)
    score(FAR, 0, 4)

    back = [copy_to(sib_out.at[s], sib_in.at[s], sibling) for s in range(4)]
    held = {}

    def start_text(s):
        with jax.named_scope(f"text_{s}"):
            part = jnp.dot(coef[pl.ds(s * 2 * rows, 2 * rows), :], ib[...].reshape(4 * rows, width),
                           preferred_element_type=F32)
            sib_out[s] = part[rows:].astype(BF)
            back[s].start()
            held[s] = part[:rows]

    def finish_text(s):
        arrived(f"text_sibling_{s}", back[s])
        whole = held[s] + sib_in[s].astype(F32)
        if s == OWN:
            gt[...] = whole
        else:
            t_out[s - 1] = whole.astype(BF)

    def image(slot):
        with jax.named_scope(f"image_{slot}"):
            i_out[slot - 1] = image_partial(slot).astype(BF)

    f_p0 = copy_to(t_out.at[FAR - 1, h0], t_mid.at[0], pair)
    f_n1 = copy_to(t_out.at[FAR - 1, h1], t_mid.at[1], near_of)
    b_p0 = copy_to(t_out.at[PAIR - 1, h0], t_in.at[0, h0], pair)
    b_p1 = copy_to(t_out.at[PAIR - 1, h1], t_in.at[0, h1], pair)
    b_n1 = copy_to(t_out.at[NEAR - 1, h1], t_in.at[1, h1], near_of)
    b_n0 = copy_to(t_out.at[NEAR - 1, h0], t_in.at[1, h0], near_of)
    f_r0 = copy_to(i_out.at[OPP - 1, h0], i_mid.at[0], right)
    f_l1 = copy_to(i_out.at[OPP - 1, h1], i_mid.at[1], left)
    b_r1 = copy_to(i_out.at[RIGHT - 1, h1], i_in.at[0, h1], right)
    b_r0 = copy_to(i_out.at[RIGHT - 1, h0], i_in.at[0, h0], right)
    b_l0 = copy_to(i_out.at[LEFT - 1, h0], i_in.at[1, h0], left)
    b_l1 = copy_to(i_out.at[LEFT - 1, h1], i_in.at[1, h1], left)
    l_o = copy_to(loss.at[OPP], l_mid, right)
    l_r = copy_to(loss.at[RIGHT], l_in.at[0], right)
    l_l = copy_to(loss.at[LEFT], l_in.at[1], left)

    l_o.start()
    start_text(FAR)
    image(OPP)
    f_r0.start()
    f_l1.start()
    l_l.start()
    finish_text(FAR)
    f_p0.start()
    f_n1.start()
    image(RIGHT)
    b_r1.start()
    image(LEFT)
    b_l0.start()
    start_text(PAIR)
    start_text(NEAR)
    finish_text(PAIR)
    b_p0.start()
    finish_text(NEAR)
    b_n1.start()
    start_text(OWN)
    with jax.named_scope("image_0"):
        gi[...] = image_partial(0)

    def pass_on(name, got, src, slot, part, out):
        arrived(name, got)
        src[slot, part] = (src[slot, part].astype(F32) + out[0][out[1]].astype(F32)).astype(BF)

    arrived("mid_loss", l_o)
    loss[RIGHT] += l_mid[...]
    l_r.start()
    pass_on("mid_r", f_r0, i_out, RIGHT - 1, h0, (i_mid, 0))
    b_r0.start()
    pass_on("mid_l", f_l1, i_out, LEFT - 1, h1, (i_mid, 1))
    b_l1.start()
    pass_on("mid_n", f_p0, t_out, NEAR - 1, h0, (t_mid, 0))
    b_n0.start()
    pass_on("mid_p", f_n1, t_out, PAIR - 1, h1, (t_mid, 1))
    b_p1.start()
    finish_text(OWN)

    def backnorm(values, inverse, grad):
        unit = values * inverse
        return inverse * (grad - unit * jnp.sum(unit * grad, axis=1, keepdims=True))

    arrived("loss", l_r, l_l)
    total = loss[0] + l_in[0] + l_in[1]
    loss_ref[...] = jnp.sum(total, axis=0, keepdims=True) / mean

    arrived("image_back", b_r1, b_l0, b_r0, b_l1)
    grad = gi[...] + i_in[0].astype(F32) + i_in[1].astype(F32)
    gi[...] = backnorm(img[...], inv_i, grad)
    put_i = pltpu.make_async_copy(gi, gi_hbm, lsem.at[0])
    put_i.start()
    arrived("text_back", b_p0, b_n1, b_n0, b_p1)
    grad = gt[...] + t_in[0].astype(F32) + t_in[1].astype(F32)
    gt[...] = backnorm(txt[...], inv_t, grad)
    put_t = pltpu.make_async_copy(gt, gt_hbm, lsem.at[1])
    put_t.start()
    with jax.named_scope("sends_end"):
        for c in sent:
            c.wait_send()
    with jax.named_scope("put"):
        put_i.wait()
        put_t.wait()


def body(images, texts, log_scale, bias):
    rows, width = images.shape
    n_blk = lax.axis_size("blk")
    mean = STEPS * rows * lax.axis_size("grp")
    low = functools.partial(pltpu.VMEM, dtype=BF)
    full = functools.partial(pltpu.VMEM, dtype=F32)
    any_space = pl.BlockSpec(memory_space=pl.ANY)
    row_loss, image_grad, text_grad = pl.pallas_call(
        functools.partial(kernel, n_blk, mean),
        out_shape=(
            jax.ShapeDtypeStruct((1, rows), F32),
            jax.ShapeDtypeStruct((rows, width), F32),
            jax.ShapeDtypeStruct((rows, width), F32),
        ),
        in_specs=[pl.BlockSpec(memory_space=pltpu.SMEM)] * 2 + [any_space] * 2,
        out_specs=(pl.BlockSpec(memory_space=pltpu.VMEM), any_space, any_space),
        scratch_shapes=[
            full((rows, width)), full((rows, width)), full((rows, width)), full((rows, width)),
            low((4, rows, width)),
            low((4, 2, rows, width)),
            low((8 * rows, 4 * rows)),
            full((4, 8, rows)),
            low((4, rows, width)), low((4, rows, width)),
            low((3, rows, width)), low((2, rows // 2, width)), low((2, rows, width)),
            low((3, rows, width)), low((2, rows // 2, width)), low((2, rows, width)),
            full((8, rows)), full((2, 8, rows)),
            pltpu.SemaphoreType.DMA((2,)),
            pltpu.SemaphoreType.DMA((N_SEMS,)),
            pltpu.SemaphoreType.DMA((N_SEMS,)),
        ],
        compiler_params=pltpu.CompilerParams(
            collective_id=0, has_side_effects=True, vmem_limit_bytes=62 << 20),
        name="pair_loss",
    )(log_scale, bias, images, texts)
    return row_loss.reshape(rows), image_grad, text_grad


def solution(mesh):
    in_specs = (P(("blk", "grp"), None), P(("blk", "grp"), None), P(), P())
    out_specs = (P(("blk", "grp")), P(("blk", "grp"), None), P(("blk", "grp"), None))
    return jax.shard_map(body, mesh=mesh, in_specs=in_specs, out_specs=out_specs, check_vma=False)
```

```python
import functools

import jax
import jax.numpy as jnp
from jax import lax
from jax.experimental import pallas as pl
from jax.experimental.pallas import tpu as pltpu
from jax.sharding import PartitionSpec as P

STEPS = 2
MESH = pl.DeviceIdType.MESH
BF = jnp.bfloat16
F32 = jnp.float32
N_SEMS = 38
GROUP = 16
PARTS = 4

OWN, PAIR, NEAR, FAR = 0, 1, 2, 3
RIGHT, LEFT, OPP = 1, 2, 3


def places(n_blk):
    b = lax.axis_index("blk")
    g = lax.axis_index("grp")
    core = lax.rem(g, 2)
    x_lo = lax.rem(g // 2, 2)
    y = g // 4
    nxt = lax.rem(b + 1, n_blk)
    prv = lax.rem(b + n_blk - 1, n_blk)

    def member(yy, xx, kk):
        return (yy * 2 + xx) * 2 + kk

    sibling = (b, member(y, x_lo, 1 - core))
    pair = (b, member(y, 1 - x_lo, core))
    near_to = (nxt, member(y, 1 - x_lo, core))
    near_of = (prv, member(y, 1 - x_lo, core))
    right = (b, member(lax.rem(y + 1, 4), x_lo, core))
    left = (b, member(lax.rem(y + 3, 4), x_lo, core))
    return sibling, pair, near_to, near_of, right, left


def inverse_norm(values):
    return lax.rsqrt(jnp.sum(values * values, axis=1, keepdims=True) + 1e-06)


def kernel(n_blk, mean, ls_hbm, bi_hbm, img_hbm, txt_hbm, loss_hbm, gi_hbm, gt_hbm,
           ls_ref, bi_ref, img, txt, gi, gt, row, ib, tb, tf, coef, coef_f, loss, sib_out, sib_in,
           t_out, t_mid, t_in, i_out, i_mid, i_in, l_mid, l_in, lsem, ssem, rsem):
    rows, width = img.shape
    half = rows // 2
    h0, h1 = pl.ds(0, half), pl.ds(half, half)
    sibling, pair, near_to, near_of, right, left = places(n_blk)
    load_t = pltpu.make_async_copy(txt_hbm, txt, lsem.at[0])
    load_i = pltpu.make_async_copy(img_hbm, img, lsem.at[1])
    load_t.start()
    load_i.start()
    load_s = pltpu.make_async_copy(ls_hbm, ls_ref, lsem.at[2])
    load_b = pltpu.make_async_copy(bi_hbm, bi_ref, lsem.at[3])
    load_s.start()
    load_b.start()

    barrier = pltpu.get_barrier_semaphore()
    others = [sibling, pair, near_of, right, left]
    for other in others:
        pl.semaphore_signal(barrier, inc=1, device_id=other, device_id_type=MESH)

    sent = []

    def copy_to(src, dst, to):
        s = len(sent)
        copy = pltpu.make_async_remote_copy(
            src_ref=src, dst_ref=dst, send_sem=ssem.at[s], recv_sem=rsem.at[s],
            device_id=to, device_id_type=MESH)
        sent.append(copy)
        return copy

    def arrived(name, *copies):
        with jax.named_scope("wait_" + name):
            for c in copies:
                c.wait_recv()

    with jax.named_scope("normalize"):
        load_t.wait()
        inv_t = inverse_norm(txt[...])
        tb[0, OWN] = (txt[...] * inv_t).astype(BF)
        load_i.wait()
        inv_i = inverse_norm(img[...])
        ib[0] = (img[...] * inv_i).astype(BF)
    with jax.named_scope("barrier"):
        pl.semaphore_wait(barrier, len(others))

    t_p0 = copy_to(tb.at[0, OWN, h0], tb.at[0, PAIR, h0], pair)
    t_n1 = copy_to(tb.at[0, OWN, h1], tb.at[0, NEAR, h1], near_to)
    i_r0 = copy_to(ib.at[0, h0], ib.at[LEFT, h0], right)
    i_l1 = copy_to(ib.at[0, h1], ib.at[RIGHT, h1], left)
    t_p1 = copy_to(tb.at[0, OWN, h1], tb.at[0, PAIR, h1], pair)
    t_n0 = copy_to(tb.at[0, OWN, h0], tb.at[0, NEAR, h0], near_to)
    i_r1 = copy_to(ib.at[0, h1], ib.at[LEFT, h1], right)
    i_l0 = copy_to(ib.at[0, h0], ib.at[RIGHT, h0], left)
    s_own = copy_to(tb.at[0, OWN], tb.at[1, OWN], sibling)
    for c in sent:
        c.start()
    t_f0 = copy_to(tb.at[0, PAIR, h0], tf.at[0, h0], near_to)
    t_f1 = copy_to(tb.at[0, NEAR, h1], tf.at[0, h1], pair)
    i_o0 = copy_to(ib.at[LEFT, h0], ib.at[OPP, h0], right)
    i_o1 = copy_to(ib.at[RIGHT, h1], ib.at[OPP, h1], left)
    s_p0 = copy_to(tb.at[0, PAIR, h0], tb.at[1, PAIR, h0], sibling)
    s_n1 = copy_to(tb.at[0, NEAR, h1], tb.at[1, NEAR, h1], sibling)
    s_p1 = copy_to(tb.at[0, PAIR, h1], tb.at[1, PAIR, h1], sibling)
    s_n0 = copy_to(tb.at[0, NEAR, h0], tb.at[1, NEAR, h0], sibling)
    s_f0 = copy_to(tf.at[0, h0], tf.at[1, h0], sibling)
    s_f1 = copy_to(tf.at[0, h1], tf.at[1, h1], sibling)

    load_s.wait()
    load_b.wait()
    temper = jnp.exp(jnp.full((1, 1), ls_ref[0], F32))
    offset = bi_ref[0]
    loss[...] = jnp.zeros_like(loss)

    def score(name, chunk, weights, lo, hi, pairs=False):
        with jax.named_scope("score_" + name):
            n, m = chunk.shape[0], (hi - lo) * rows
            dots = lax.dot_general(chunk, ib[lo:hi].reshape(m, width),
                                   (((1,), (1,)), ((), ())), preferred_element_type=F32)
            logit = temper * dots + offset
            e = jnp.exp(-jnp.abs(logit))
            weight = jnp.where(logit >= 0, 1.0, e) * pl.reciprocal(1.0 + e, approx=True)
            signed = logit
            if pairs:
                r = lax.broadcasted_iota(jnp.int32, logit.shape, 0)
                paired = (r == lax.broadcasted_iota(jnp.int32, logit.shape, 1)) & (r < rows)
                weight = weight - paired.astype(F32)
                signed = jnp.where(paired, -logit, logit)
            weights[:, pl.ds(lo * rows, m)] = (temper * weight).astype(BF)
            e = e.reshape(n // (8 * GROUP), GROUP, 8, m)
            p = e[:, 0]
            for g in range(1, GROUP):
                p = p + e[:, g] * (1.0 + p)
            log1p = jnp.where(p < 1e-3, p * (1.0 - 0.5 * p), jnp.log(1.0 + p))
            lost = (jnp.sum(jnp.maximum(signed, 0.0).reshape(n // 8, 8, m), axis=0)
                    + jnp.sum(log1p, axis=0))
            for slot in range(lo, hi):
                loss[slot] += lost[:, (slot - lo) * rows:(slot - lo + 1) * rows]

    def score_main(kk, lo, hi):
        score(f"main_{kk}_{lo}_{hi}", tb[kk].reshape(3 * rows, width),
              coef.at[pl.ds(kk * 3 * rows, 3 * rows)], lo, hi, pairs=kk == 0 and lo == 0)

    def score_far(kk):
        score(f"far_{kk}", tf[kk], coef_f.at[pl.ds(kk * rows, rows)], 0, OPP + 1)

    def image_partial(lo, hi):
        turned = (((0,), (0,)), ((), ()))
        cols = pl.ds(lo * rows, (hi - lo) * rows)
        return (lax.dot_general(coef[:, cols], tb[...].reshape(6 * rows, width), turned,
                                preferred_element_type=F32)
                + lax.dot_general(coef_f[:, cols], tf[...].reshape(2 * rows, width), turned,
                                  preferred_element_type=F32))

    arrived("first_p", t_p0)
    t_f0.start()
    s_p0.start()
    arrived("first_i", i_r0, i_l1)
    i_o0.start()
    i_o1.start()
    arrived("first_n", t_n1)
    t_f1.start()
    s_n1.start()
    arrived("second_p", t_p1)
    s_p1.start()
    arrived("second_n", t_n0)
    s_n0.start()
    arrived("second_i", i_r1, i_l0)
    score_main(0, 0, OPP)
    arrived("main_sibling", s_own, s_p0, s_n1, s_p1, s_n0)
    score_main(1, 0, OPP)
    arrived("opp_i", i_o0, i_o1)
    score_main(0, OPP, OPP + 1)
    score_main(1, OPP, OPP + 1)
    arrived("far_t0", t_f0)
    s_f0.start()
    arrived("far_t1", t_f1)
    s_f1.start()
    score_far(0)
    arrived("far_sibling", s_f0, s_f1)
    score_far(1)

    back = [copy_to(sib_out.at[s], sib_in.at[s], sibling) for s in range(4)]
    f_p0 = copy_to(t_out.at[FAR - 1, h0], t_mid.at[0], pair)
    f_n1 = copy_to(t_out.at[FAR - 1, h1], t_mid.at[1], near_of)
    b_p0 = copy_to(t_out.at[PAIR - 1, h0], t_in.at[0, h0], pair)
    b_p1 = copy_to(t_out.at[PAIR - 1, h1], t_in.at[0, h1], pair)
    b_n1 = copy_to(t_out.at[NEAR - 1, h1], t_in.at[1, h1], near_of)
    b_n0 = copy_to(t_out.at[NEAR - 1, h0], t_in.at[1, h0], near_of)
    f_r0 = copy_to(i_out.at[OPP - 1, h0], i_mid.at[0], right)
    f_l1 = copy_to(i_out.at[OPP - 1, h1], i_mid.at[1], left)
    b_r1 = copy_to(i_out.at[RIGHT - 1, h1], i_in.at[0, h1], right)
    b_r0 = copy_to(i_out.at[RIGHT - 1, h0], i_in.at[0, h0], right)
    b_l0 = copy_to(i_out.at[LEFT - 1, h0], i_in.at[1, h0], left)
    b_l1 = copy_to(i_out.at[LEFT - 1, h1], i_in.at[1, h1], left)
    l_o = copy_to(loss.at[OPP], l_mid, right)
    l_r = copy_to(loss.at[RIGHT], l_in.at[0], right)
    l_l = copy_to(loss.at[LEFT], l_in.at[1], left)

    all_images = ib[...].reshape(4 * rows, width)

    def text_partial(weights):
        return jnp.dot(weights, all_images, preferred_element_type=F32)

    def add_sibling(s, part):
        arrived(f"text_sibling_{s}", back[s])
        return part + sib_in[s].astype(F32)

    l_o.start()
    with jax.named_scope("image_opp"):
        i_out[OPP - 1] = image_partial(OPP, OPP + 1).astype(BF)
        f_r0.start()
        f_l1.start()
    with jax.named_scope("text_far_1"):
        sib_out[FAR] = text_partial(coef_f[rows:]).astype(BF)
        back[FAR].start()
    l_l.start()
    with jax.named_scope("text_far_0"):
        far = text_partial(coef_f[:rows])
    t_out[FAR - 1] = add_sibling(FAR, far).astype(BF)
    f_p0.start()
    f_n1.start()
    with jax.named_scope("text_main_1"):
        sib_out[OWN:FAR] = text_partial(coef[3 * rows:]).astype(BF).reshape(3, rows, width)
        for s in (PAIR, NEAR, OWN):
            back[s].start()
    with jax.named_scope("image_next"):
        i_out[RIGHT - 1:LEFT] = image_partial(RIGHT, LEFT + 1).astype(BF).reshape(2, rows, width)
        b_r1.start()
        b_l0.start()
    with jax.named_scope("text_main_0"):
        main = text_partial(coef[:3 * rows])
        gt[...] = main[:rows]
    t_out[PAIR - 1] = add_sibling(PAIR, main[rows:2 * rows]).astype(BF)
    b_p0.start()
    t_out[NEAR - 1] = add_sibling(NEAR, main[2 * rows:]).astype(BF)
    b_n1.start()
    with jax.named_scope("image_own"):
        gi[...] = image_partial(0, 1)

    def pass_on(name, got, src, slot, part, middle):
        arrived(name, got)
        src[slot, part] = (src[slot, part].astype(F32) + middle[...].astype(F32)).astype(BF)

    arrived("mid_loss", l_o)
    loss[RIGHT] += l_mid[...]
    l_r.start()
    pass_on("mid_r", f_r0, i_out, RIGHT - 1, h0, i_mid.at[0])
    b_r0.start()
    pass_on("mid_l", f_l1, i_out, LEFT - 1, h1, i_mid.at[1])
    b_l1.start()
    pass_on("mid_n", f_p0, t_out, NEAR - 1, h0, t_mid.at[0])
    b_n0.start()
    pass_on("mid_p", f_n1, t_out, PAIR - 1, h1, t_mid.at[1])
    b_p1.start()
    gt[...] = add_sibling(OWN, gt[...])

    def backnorm(values, inverse, grad):
        unit = values * inverse
        return inverse * (grad - unit * jnp.sum(unit * grad, axis=1, keepdims=True))

    arrived("loss", l_r, l_l)
    total = loss[0] + l_in[0] + l_in[1]
    row[...] = jnp.sum(total, axis=0, keepdims=True) / mean
    puts = [pltpu.make_async_copy(held, out, lsem.at[i])
            for i, (held, out) in enumerate(((row, loss_hbm), (gi, gi_hbm), (gt, gt_hbm)))]
    puts[0].start()
    arrived("image_back", b_r1, b_l0, b_r0, b_l1)
    with jax.named_scope("image_norm"):
        grad = gi[...] + i_in[0].astype(F32) + i_in[1].astype(F32)
        gi[...] = backnorm(img[...], inv_i, grad)
        puts[1].start()
    arrived("text_back", b_p0, b_n1, b_n0, b_p1)
    with jax.named_scope("text_norm"):
        grad = gt[...] + t_in[0].astype(F32) + t_in[1].astype(F32)
        gt[...] = backnorm(txt[...], inv_t, grad)
        puts[2].start()
    with jax.named_scope("sends_end"):
        for c in sent:
            c.wait_send()
    with jax.named_scope("put"):
        for c in puts:
            c.wait()


def hand_on(row, gi, gt, row_out, gi_out, gt_out, row_held, gi_held, gt_held, in_sem, out_sem):
    parts = [(row, row_held, row_out)]
    size = gi.shape[0] // PARTS
    for at in range(0, gi.shape[0], size):
        for src, held, out in ((gi, gi_held, gi_out), (gt, gt_held, gt_out)):
            parts.append(tuple(ref.at[pl.ds(at, size)] for ref in (src, held, out)))
    reads = [pltpu.make_async_copy(src, held, in_sem.at[i]) for i, (src, held, _) in enumerate(parts)]
    writes = [pltpu.make_async_copy(held, out, out_sem.at[i]) for i, (_, held, out) in enumerate(parts)]
    for c in reads:
        c.start()
    for r, w in zip(reads, writes):
        r.wait()
        w.start()
    for c in writes:
        c.wait()


def body(images, texts, log_scale, bias):
    rows, width = images.shape
    n_blk = lax.axis_size("blk")
    mean = STEPS * rows * lax.axis_size("grp")
    low = functools.partial(pltpu.VMEM, dtype=BF)
    full = functools.partial(pltpu.VMEM, dtype=F32)
    anywhere = pl.BlockSpec(memory_space=pl.ANY)
    results = (
        jax.ShapeDtypeStruct((1, rows), F32),
        jax.ShapeDtypeStruct((rows, width), F32),
        jax.ShapeDtypeStruct((rows, width), F32),
    )
    held = pl.pallas_call(
        functools.partial(kernel, n_blk, mean),
        out_shape=results,
        in_specs=[anywhere] * 4,
        out_specs=(anywhere,) * 3,
        scratch_shapes=[
            pltpu.SMEM((1,), F32), pltpu.SMEM((1,), F32),
            full((rows, width)), full((rows, width)),
            full((rows, width)), full((rows, width)), full((1, rows)),
            low((4, rows, width)),
            low((2, 3, rows, width)), low((2, rows, width)),
            low((6 * rows, 4 * rows)), low((2 * rows, 4 * rows)),
            full((4, 8, rows)),
            low((4, rows, width)), low((4, rows, width)),
            low((3, rows, width)), low((2, rows // 2, width)), low((2, rows, width)),
            low((3, rows, width)), low((2, rows // 2, width)), low((2, rows, width)),
            full((8, rows)), full((2, 8, rows)),
            pltpu.SemaphoreType.DMA((4,)),
            pltpu.SemaphoreType.DMA((N_SEMS,)),
            pltpu.SemaphoreType.DMA((N_SEMS,)),
        ],
        compiler_params=pltpu.CompilerParams(
            collective_id=0, has_side_effects=True, vmem_limit_bytes=(64 << 20) - (1 << 19)),
        name="pair_loss",
    )(log_scale, bias, images, texts)
    row_loss, image_grad, text_grad = pl.pallas_call(
        hand_on,
        out_shape=results,
        in_specs=[anywhere] * 3,
        out_specs=(anywhere,) * 3,
        scratch_shapes=[
            full((1, rows)), full((rows, width)), full((rows, width)),
            pltpu.SemaphoreType.DMA((2 * PARTS + 1,)), pltpu.SemaphoreType.DMA((2 * PARTS + 1,)),
        ],
        name="hand_on",
    )(*held)
    return row_loss.reshape(rows), image_grad, text_grad


def solution(mesh):
    in_specs = (P(("blk", "grp"), None), P(("blk", "grp"), None), P(), P())
    out_specs = (P(("blk", "grp")), P(("blk", "grp"), None), P(("blk", "grp"), None))
    return jax.shard_map(body, mesh=mesh, in_specs=in_specs, out_specs=out_specs, check_vma=False)
```

```python
import functools

import jax
import jax.numpy as jnp
from jax import lax
from jax.experimental import pallas as pl
from jax.experimental.pallas import tpu as pltpu
from jax.sharding import PartitionSpec as P

STEPS = 2
MESH = pl.DeviceIdType.MESH
BF = jnp.bfloat16
F32 = jnp.float32
N_SEMS = 44
GROUP = 16
PARTS = 4

OWN0, PAIR0, OWN1, PAIR1, NEAR0, NEAR1, FAR0, FAR1 = range(8)
OWN, PAIR, NEAR, FAR = range(4)
RIGHT, LEFT, OPP = 1, 2, 3


def places(n_blk):
    b = lax.axis_index("blk")
    g = lax.axis_index("grp")
    core = lax.rem(g, 2)
    x_lo = lax.rem(g // 2, 2)
    y = g // 4
    nxt = lax.rem(b + 1, n_blk)
    prv = lax.rem(b + n_blk - 1, n_blk)

    def member(yy, xx, kk):
        return (yy * 2 + xx) * 2 + kk

    sibling = (b, member(y, x_lo, 1 - core))
    pair = (b, member(y, 1 - x_lo, core))
    near_to = (nxt, member(y, 1 - x_lo, core))
    near_of = (prv, member(y, 1 - x_lo, core))
    right = (b, member(lax.rem(y + 1, 4), x_lo, core))
    left = (b, member(lax.rem(y + 3, 4), x_lo, core))
    return sibling, pair, near_to, near_of, right, left


def inverse_norm(values):
    return lax.rsqrt(jnp.sum(values * values, axis=1, keepdims=True) + 1e-06)


def kernel(n_blk, mean, ls_hbm, bi_hbm, img_hbm, txt_hbm, loss_hbm, gi_hbm, gt_hbm,
           ls_ref, bi_ref, img, txt, gi, gt, row, kept, ib, tb, coef, loss, sib_out, sib_in,
           t_out, t_mid, t_in, i_out, i_mid, i_in, l_mid, l_in, lsem, ssem, rsem):
    rows, width = img.shape
    half = rows // 2
    h0, h1 = pl.ds(0, half), pl.ds(half, half)
    quarters = [pl.ds(at, half // 2) for at in range(0, rows, half // 2)]
    blk = lax.axis_index("blk")
    sibling, pair, near_to, near_of, right, left = places(n_blk)
    barrier = pltpu.get_barrier_semaphore()
    others = [sibling, pair, near_of, right, left]
    for other in others:
        pl.semaphore_signal(barrier, inc=1, device_id=other, device_id_type=MESH)

    load_t = pltpu.make_async_copy(txt_hbm, txt, lsem.at[0])
    load_i = pltpu.make_async_copy(img_hbm, img, lsem.at[1])
    load_t.start()
    load_i.start()
    load_s = pltpu.make_async_copy(ls_hbm, ls_ref, lsem.at[2])
    load_b = pltpu.make_async_copy(bi_hbm, bi_ref, lsem.at[3])
    load_s.start()
    load_b.start()

    sent = []

    def copy_to(src, dst, to):
        s = len(sent)
        copy = pltpu.make_async_remote_copy(
            src_ref=src, dst_ref=dst, send_sem=ssem.at[s], recv_sem=rsem.at[s],
            device_id=to, device_id_type=MESH)
        sent.append(copy)
        return copy

    def arrived(name, *copies):
        with jax.named_scope("wait_" + name):
            for c in copies:
                c.wait_recv()

    with jax.named_scope("normalize_text"):
        load_t.wait()
        inv_t = inverse_norm(txt[...])
        tb[OWN0] = (txt[...] * inv_t).astype(BF)
    with jax.named_scope("barrier"):
        pl.semaphore_wait(barrier, len(others))

    t_p0 = copy_to(tb.at[OWN0, h0], tb.at[PAIR0, h0], pair)
    t_n = [copy_to(tb.at[OWN0, q], tb.at[NEAR0, q], near_to) for q in quarters]
    t_p1 = copy_to(tb.at[OWN0, h1], tb.at[PAIR0, h1], pair)
    s_own = copy_to(tb.at[OWN0], tb.at[OWN1], sibling)
    for c in (t_n[3], t_p0, t_n[2], t_p1, t_n[1], t_n[0], s_own):
        c.start()
    with jax.named_scope("normalize_image"):
        load_i.wait()
        inv_i = inverse_norm(img[...])
        ib[0] = (img[...] * inv_i).astype(BF)
    i_r0 = copy_to(ib.at[0, h0], ib.at[LEFT, h0], right)
    i_l1 = copy_to(ib.at[0, h1], ib.at[RIGHT, h1], left)
    i_r1 = copy_to(ib.at[0, h1], ib.at[LEFT, h1], right)
    i_l0 = copy_to(ib.at[0, h0], ib.at[RIGHT, h0], left)
    for c in (i_r0, i_l1, i_r1, i_l0):
        c.start()
    i_o0 = copy_to(ib.at[LEFT, h0], ib.at[OPP, h0], right)
    i_o1 = copy_to(ib.at[RIGHT, h1], ib.at[OPP, h1], left)
    s_p0 = copy_to(tb.at[PAIR0, h0], tb.at[PAIR1, h0], sibling)
    s_n1 = copy_to(tb.at[NEAR0, h1], tb.at[NEAR1, h1], sibling)
    s_p1 = copy_to(tb.at[PAIR0, h1], tb.at[PAIR1, h1], sibling)
    s_n0 = copy_to(tb.at[NEAR0, h0], tb.at[NEAR1, h0], sibling)
    s_f0 = copy_to(tb.at[FAR0, h0], tb.at[FAR1, h0], sibling)
    s_f1 = copy_to(tb.at[FAR0, h1], tb.at[FAR1, h1], sibling)
    t_f0 = copy_to(tb.at[PAIR0, h0], tb.at[FAR0, h0], near_to)
    t_f1 = copy_to(tb.at[NEAR0, h1], tb.at[FAR0, h1], pair)
    t_q = ([copy_to(tb.at[PAIR0, quarters[0]], tb.at[FAR0, quarters[0]], near_to)]
           + [copy_to(tb.at[NEAR0, q], tb.at[FAR0, q], pair) for q in quarters[1:]])
    into_first = blk == n_blk - 1
    first = blk == 0

    load_s.wait()
    load_b.wait()
    temper = jnp.exp(jnp.full((1, 1), ls_ref[0], F32))
    offset = bi_ref[0]
    loss[...] = jnp.zeros_like(loss)

    def score(first, last, lo, hi):
        with jax.named_scope(f"score_{first}_{last}_{lo}_{hi}"):
            n, m = (last - first) * rows, (hi - lo) * rows
            dots = lax.dot_general(tb[first:last].reshape(n, width), ib[lo:hi].reshape(m, width),
                                   (((1,), (1,)), ((), ())), preferred_element_type=F32)
            logit = temper * dots + offset
            e = jnp.exp(-jnp.abs(logit))
            weight = jnp.where(logit >= 0, 1.0, e) * pl.reciprocal(1.0 + e, approx=True)
            signed = logit
            if first == OWN0 and lo == 0:
                r = lax.broadcasted_iota(jnp.int32, logit.shape, 0)
                paired = (r == lax.broadcasted_iota(jnp.int32, logit.shape, 1)) & (r < rows)
                weight = weight - paired.astype(F32)
                signed = jnp.where(paired, -logit, logit)
            coef[pl.ds(first * rows, n), pl.ds(lo * rows, m)] = (temper * weight).astype(BF)
            e = e.reshape(n // (8 * GROUP), GROUP, 8, m)
            p = e[:, 0]
            for g in range(1, GROUP):
                p = p + e[:, g] * (1.0 + p)
            log1p = jnp.where(p < 1e-3, p * (1.0 - 0.5 * p), jnp.log(1.0 + p))
            lost = (jnp.sum(jnp.maximum(signed, 0.0).reshape(n // 8, 8, m), axis=0)
                    + jnp.sum(log1p, axis=0))
            for slot in range(lo, hi):
                loss[slot] += lost[:, (slot - lo) * rows:(slot - lo + 1) * rows]

    def image_partial(lo, hi, first, last):
        return lax.dot_general(coef[first * rows:last * rows, lo * rows:hi * rows],
                               tb[first:last].reshape((last - first) * rows, width),
                               (((0,), (0,)), ((), ())), preferred_element_type=F32)

    back = [copy_to(sib_out.at[s], sib_in.at[s], sibling) for s in range(4)]
    f_p0 = copy_to(t_out.at[FAR - 1, h0], t_mid.at[0], pair)
    f_n1 = copy_to(t_out.at[FAR - 1, h1], t_mid.at[1], near_of)
    b_p0 = copy_to(t_out.at[PAIR - 1, h0], t_in.at[0, h0], pair)
    b_p1 = copy_to(t_out.at[PAIR - 1, h1], t_in.at[0, h1], pair)
    b_n1 = copy_to(t_out.at[NEAR - 1, h1], t_in.at[1, h1], near_of)
    b_n0 = copy_to(t_out.at[NEAR - 1, h0], t_in.at[1, h0], near_of)
    f_r0 = copy_to(i_out.at[OPP - 1, h0], i_mid.at[0], right)
    f_l1 = copy_to(i_out.at[OPP - 1, h1], i_mid.at[1], left)
    b_r1 = copy_to(i_out.at[RIGHT - 1, h1], i_in.at[0, h1], right)
    b_r0 = copy_to(i_out.at[RIGHT - 1, h0], i_in.at[0, h0], right)
    b_l0 = copy_to(i_out.at[LEFT - 1, h0], i_in.at[1, h0], left)
    b_l1 = copy_to(i_out.at[LEFT - 1, h1], i_in.at[1, h1], left)
    l_o = copy_to(loss.at[OPP], l_mid, right)
    l_r = copy_to(loss.at[RIGHT], l_in.at[0], right)
    l_l = copy_to(loss.at[LEFT], l_in.at[1], left)

    def text_partial(first, last):
        return jnp.dot(coef[first * rows:last * rows], ib[...].reshape(4 * rows, width),
                       preferred_element_type=F32)

    def to_sibling(s, part):
        sib_out[s] = part.astype(BF)
        back[s].start()

    def add_sibling(s, part):
        arrived(f"text_sibling_{s}", back[s])
        return part + sib_in[s].astype(F32)

    def pass_on(name, got, src, slot, part, middle, out):
        arrived(name, got)
        src[slot, part] = (src[slot, part].astype(F32) + middle[...].astype(F32)).astype(BF)
        out.start()

    def pass_loss():
        arrived("mid_loss", l_o)
        loss[RIGHT] += l_mid[...]
        l_r.start()

    def pass_right():
        pass_on("mid_r", f_r0, i_out, RIGHT - 1, h0, i_mid.at[0], b_r0)

    def pass_left():
        pass_on("mid_l", f_l1, i_out, LEFT - 1, h1, i_mid.at[1], b_l1)

    def pass_near():
        pass_on("mid_n", f_p0, t_out, NEAR - 1, h0, t_mid.at[0], b_n0)

    def pass_pair():
        pass_on("mid_p", f_n1, t_out, PAIR - 1, h1, t_mid.at[1], b_p1)

    puts = [pltpu.make_async_copy(held, out, lsem.at[i])
            for i, (held, out) in enumerate(((row, loss_hbm), (gi, gi_hbm), (gt, gt_hbm)))]

    def backnorm(values, inverse, grad):
        unit = values * inverse
        return inverse * (grad - unit * jnp.sum(unit * grad, axis=1, keepdims=True))

    def finish_loss():
        arrived("loss", l_r, l_l)
        total = loss[0] + l_in[0] + l_in[1]
        row[...] = jnp.sum(total, axis=0, keepdims=True) / mean
        puts[0].start()

    def finish_image():
        arrived("image_back", b_r1, b_l0, b_r0, b_l1)
        with jax.named_scope("image_norm"):
            grad = gi[...] + i_in[0].astype(F32) + i_in[1].astype(F32)
            gi[...] = backnorm(img[...], inv_i, grad)
            puts[1].start()

    def finish_text():
        arrived("text_back", b_p0, b_n1, b_n0, b_p1)
        with jax.named_scope("text_norm"):
            grad = gt[...] + t_in[0].astype(F32) + t_in[1].astype(F32)
            gt[...] = backnorm(txt[...], inv_t, grad)
            puts[2].start()

    def start_own_plane():
        arrived("first_p", t_p0)
        pl.when(into_first)(t_q[0].start)
        pl.when(jnp.logical_not(into_first))(t_f0.start)
        s_p0.start()
        arrived("first_i", i_r0, i_l1)
        i_o0.start()
        i_o1.start()

    @pl.when(jnp.logical_not(first))
    def _():
        start_own_plane()
        arrived("first_n", t_n[3], t_n[2])
        t_f1.start()
        s_n1.start()
        arrived("second_p", t_p1)
        s_p1.start()
        arrived("second_n", t_n[1], t_n[0])
        s_n0.start()
        arrived("second_i", i_r1, i_l0)
        score(OWN0, OWN1, 0, OPP)
        arrived("pair_sibling", s_own, s_p0, s_p1)
        score(OWN1, NEAR0, 0, OPP)
        arrived("near_sibling", s_n1, s_n0)
        score(NEAR0, FAR0, 0, OPP)
        arrived("far_t0", t_f0)
        s_f0.start()
        arrived("far_t1", t_f1)
        s_f1.start()
        arrived("opp_i", i_o0, i_o1)
        score(OWN0, FAR0, OPP, OPP + 1)
        score(FAR0, FAR1, 0, OPP + 1)
        arrived("far_sibling", s_f0, s_f1)
        score(FAR1, FAR1 + 1, 0, OPP + 1)
        l_o.start()
        l_l.start()
        with jax.named_scope("text_far_1"):
            to_sibling(FAR, text_partial(FAR1, FAR1 + 1))
        with jax.named_scope("image_opp"):
            i_out[OPP - 1] = image_partial(OPP, OPP + 1, OWN0, FAR1 + 1).astype(BF)
            f_r0.start()
            f_l1.start()
        with jax.named_scope("text_far_0"):
            t_out[FAR - 1] = add_sibling(FAR, text_partial(FAR0, FAR1)).astype(BF)
            f_p0.start()
            f_n1.start()
        with jax.named_scope("text_mid"):
            mid = text_partial(OWN1, FAR0)
            to_sibling(PAIR, mid[rows:2 * rows])
            to_sibling(NEAR, mid[3 * rows:])
            to_sibling(OWN, mid[:rows])
            near = mid[2 * rows:3 * rows]
        with jax.named_scope("image_next"):
            part = image_partial(RIGHT, LEFT + 1, OWN0, FAR1 + 1)
            i_out[RIGHT - 1:LEFT] = part.astype(BF).reshape(2, rows, width)
            b_r1.start()
            b_l0.start()
        with jax.named_scope("text_near"):
            t_out[NEAR - 1] = add_sibling(NEAR, near).astype(BF)
            b_n1.start()
        with jax.named_scope("text_own"):
            own = text_partial(OWN0, OWN1)
            t_out[PAIR - 1] = add_sibling(PAIR, own[rows:]).astype(BF)
            b_p0.start()
            gt[...] = own[:rows]
        with jax.named_scope("image_own"):
            gi[...] = image_partial(0, 1, OWN0, FAR1 + 1)
        pass_loss()
        pass_right()
        pass_left()
        pass_near()
        pass_pair()
        gt[...] = add_sibling(OWN, gt[...])
        finish_loss()
        finish_image()
        finish_text()

    @pl.when(first)
    def _():
        start_own_plane()
        arrived("second_p", t_p1)
        s_p1.start()
        arrived("second_i", i_r1, i_l0)
        score(OWN0, OWN1, 0, OPP)
        arrived("pair_sibling", s_own, s_p0, s_p1)
        score(OWN1, NEAR0, 0, OPP)
        arrived("opp_i", i_o0, i_o1)
        score(OWN0, NEAR0, OPP, OPP + 1)
        arrived("first_n", t_n[3])
        t_q[3].start()
        arrived("second_n", t_n[2])
        t_q[2].start()
        s_n1.start()
        arrived("third_n", t_n[1])
        t_q[1].start()
        with jax.named_scope("text_block"):
            part = text_partial(OWN0, NEAR0)
            to_sibling(PAIR, part[3 * rows:])
            to_sibling(OWN, part[2 * rows:3 * rows])
            gt[...] = part[:rows]
            kept[...] = part[rows:2 * rows]
        arrived("last_n", t_n[0])
        s_n0.start()
        score(NEAR0, NEAR1, 0, OPP + 1)
        arrived("near_sibling", s_n1, s_n0)
        score(NEAR1, FAR0, 0, OPP + 1)
        arrived("far_t1", t_q[3], t_q[2])
        s_f1.start()
        arrived("far_t0", t_q[0], t_q[1])
        s_f0.start()
        score(FAR0, FAR1, 0, OPP + 1)
        with jax.named_scope("image_ahead"):
            gi[...] = image_partial(OPP, OPP + 1, OWN0, FAR0)
        t_out[PAIR - 1] = add_sibling(PAIR, kept[...]).astype(BF)
        b_p0.start()
        arrived("far_sibling", s_f0, s_f1)
        score(FAR1, FAR1 + 1, 0, OPP + 1)
        l_o.start()
        l_l.start()
        with jax.named_scope("image_opp"):
            i_out[OPP - 1] = (gi[...] + image_partial(OPP, OPP + 1, FAR0, FAR1 + 1)).astype(BF)
            f_r0.start()
            f_l1.start()
        with jax.named_scope("text_far"):
            part = text_partial(NEAR0, FAR1 + 1)
            to_sibling(FAR, part[3 * rows:])
            to_sibling(NEAR, part[rows:2 * rows])
            kept[...] = part[2 * rows:3 * rows]
            near = part[:rows]
        with jax.named_scope("image_next"):
            part = image_partial(RIGHT, OPP, OWN0, FAR1 + 1)
            i_out[RIGHT - 1:LEFT] = part.astype(BF).reshape(2, rows, width)
            b_r1.start()
            b_l0.start()
        t_out[FAR - 1] = add_sibling(FAR, kept[...]).astype(BF)
        f_p0.start()
        f_n1.start()
        t_out[NEAR - 1] = add_sibling(NEAR, near).astype(BF)
        b_n1.start()
        pass_pair()
        gt[...] = add_sibling(OWN, gt[...])
        with jax.named_scope("image_own"):
            gi[...] = image_partial(0, 1, OWN0, FAR1 + 1)
        pass_loss()
        pass_right()
        pass_left()
        pass_near()
        finish_loss()
        finish_text()
        finish_image()

    with jax.named_scope("sends_end"):
        for c in sent:
            if not any(c is o for o in (t_f0, t_f1, *t_q)):
                c.wait_send()
        pl.when(into_first)(t_q[0].wait_send)
        pl.when(jnp.logical_not(into_first))(t_f0.wait_send)
        pl.when(jnp.logical_not(first))(t_f1.wait_send)
        for c in t_q[1:]:
            pl.when(first)(c.wait_send)
    with jax.named_scope("put"):
        for c in puts:
            c.wait()


def hand_on(row, gi, gt, row_out, gi_out, gt_out, row_held, gi_held, gt_held, in_sem, out_sem):
    parts = [(row, row_held, row_out)]
    size = gi.shape[0] // PARTS
    for at in range(0, gi.shape[0], size):
        for src, held, out in ((gi, gi_held, gi_out), (gt, gt_held, gt_out)):
            parts.append(tuple(ref.at[pl.ds(at, size)] for ref in (src, held, out)))
    reads = [pltpu.make_async_copy(src, held, in_sem.at[i]) for i, (src, held, _) in enumerate(parts)]
    writes = [pltpu.make_async_copy(held, out, out_sem.at[i]) for i, (_, held, out) in enumerate(parts)]
    for c in reads:
        c.start()
    for r, w in zip(reads, writes):
        r.wait()
        w.start()
    for c in writes:
        c.wait()


def body(images, texts, log_scale, bias):
    rows, width = images.shape
    n_blk = lax.axis_size("blk")
    mean = STEPS * rows * lax.axis_size("grp")
    low = functools.partial(pltpu.VMEM, dtype=BF)
    full = functools.partial(pltpu.VMEM, dtype=F32)
    anywhere = pl.BlockSpec(memory_space=pl.ANY)
    results = (
        jax.ShapeDtypeStruct((1, rows), F32),
        jax.ShapeDtypeStruct((rows, width), F32),
        jax.ShapeDtypeStruct((rows, width), F32),
    )
    held = pl.pallas_call(
        functools.partial(kernel, n_blk, mean),
        out_shape=results,
        in_specs=[anywhere] * 4,
        out_specs=(anywhere,) * 3,
        scratch_shapes=[
            pltpu.SMEM((1,), F32), pltpu.SMEM((1,), F32),
            full((rows, width)), full((rows, width)),
            full((rows, width)), full((rows, width)), full((1, rows)),
            full((rows, width)),
            low((4, rows, width)),
            low((8, rows, width)),
            low((8 * rows, 4 * rows)),
            full((4, 8, rows)),
            low((4, rows, width)), low((4, rows, width)),
            low((3, rows, width)), low((2, rows // 2, width)), low((2, rows, width)),
            low((3, rows, width)), low((2, rows // 2, width)), low((2, rows, width)),
            full((8, rows)), full((2, 8, rows)),
            pltpu.SemaphoreType.DMA((4,)),
            pltpu.SemaphoreType.DMA((N_SEMS,)),
            pltpu.SemaphoreType.DMA((N_SEMS,)),
        ],
        compiler_params=pltpu.CompilerParams(
            collective_id=0, has_side_effects=True, vmem_limit_bytes=(64 << 20) - (1 << 19)),
        name="pair_loss",
    )(log_scale, bias, images, texts)
    row_loss, image_grad, text_grad = pl.pallas_call(
        hand_on,
        out_shape=results,
        in_specs=[anywhere] * 3,
        out_specs=(anywhere,) * 3,
        scratch_shapes=[
            full((1, rows)), full((rows, width)), full((rows, width)),
            pltpu.SemaphoreType.DMA((2 * PARTS + 1,)), pltpu.SemaphoreType.DMA((2 * PARTS + 1,)),
        ],
        name="hand_on",
    )(*held)
    return row_loss.reshape(rows), image_grad, text_grad


def solution(mesh):
    in_specs = (P(("blk", "grp"), None), P(("blk", "grp"), None), P(), P())
    out_specs = (P(("blk", "grp")), P(("blk", "grp"), None), P(("blk", "grp"), None))
    return jax.shard_map(body, mesh=mesh, in_specs=in_specs, out_specs=out_specs, check_vma=False)
```

```python
import functools

import jax
import jax.numpy as jnp
from jax import lax
from jax.experimental import pallas as pl
from jax.experimental.pallas import tpu as pltpu
from jax.sharding import PartitionSpec as P

STEPS = 2
MESH = pl.DeviceIdType.MESH
BF = jnp.bfloat16
F32 = jnp.float32
N_LANDED = 30
GROUP = 16
PARTS = 4

OWN0, PAIR0, OWN1, PAIR1, NEAR0, NEAR1, FAR0, FAR1 = range(8)
OWN, PAIR, NEAR, FAR = range(4)
RIGHT, LEFT, OPP = 1, 2, 3


def places(n_blk):
    b = lax.axis_index("blk")
    g = lax.axis_index("grp")
    core = lax.rem(g, 2)
    x_lo = lax.rem(g // 2, 2)
    y = g // 4
    nxt = lax.rem(b + 1, n_blk)
    prv = lax.rem(b + n_blk - 1, n_blk)

    def member(yy, xx, kk):
        return (yy * 2 + xx) * 2 + kk

    sibling = (b, member(y, x_lo, 1 - core))
    pair = (b, member(y, 1 - x_lo, core))
    near_to = (nxt, member(y, 1 - x_lo, core))
    near_of = (prv, member(y, 1 - x_lo, core))
    right = (b, member(lax.rem(y + 1, 4), x_lo, core))
    left = (b, member(lax.rem(y + 3, 4), x_lo, core))
    return sibling, pair, near_to, near_of, right, left


def inverse_norm(values):
    return lax.rsqrt(jnp.sum(values * values, axis=1, keepdims=True) + 1e-06)


def kernel(n_blk, mean, ls_hbm, bi_hbm, img_hbm, txt_hbm, loss_hbm, gi_hbm, gt_hbm,
           ls_ref, bi_ref, img, txt, gi, gt, row, kept, ib, tb, coef, loss, sib_out, sib_in,
           t_out, t_mid, t_in, i_out, i_mid, i_in, l_mid, l_in, lsem, ssem, rsem):
    rows, width = img.shape
    half = rows // 2
    h0, h1 = pl.ds(0, half), pl.ds(half, half)
    quarters = [pl.ds(at, half // 2) for at in range(0, rows, half // 2)]
    blk = lax.axis_index("blk")
    sibling, pair, near_to, near_of, right, left = places(n_blk)
    barrier = pltpu.get_barrier_semaphore()
    others = [sibling, pair, near_of, right, left]
    for other in others:
        pl.semaphore_signal(barrier, inc=1, device_id=other, device_id_type=MESH)

    load_t = pltpu.make_async_copy(txt_hbm, txt, lsem.at[0])
    load_i = pltpu.make_async_copy(img_hbm, img, lsem.at[1])
    load_t.start()
    load_i.start()
    load_s = pltpu.make_async_copy(ls_hbm, ls_ref, lsem.at[2])
    load_b = pltpu.make_async_copy(bi_hbm, bi_ref, lsem.at[3])
    load_s.start()
    load_b.start()

    sent, landed = [], []

    def copy_to(src, dst, to, with_=None):
        if with_ is None:
            landed.append(None)
        slot = len(landed) - 1 if with_ is None else with_[1]
        copy = pltpu.make_async_remote_copy(
            src_ref=src, dst_ref=dst, send_sem=ssem.at[0], recv_sem=rsem.at[slot],
            device_id=to, device_id_type=MESH)
        sent.append(copy)
        return copy, slot

    def start(*copies):
        for c, _ in copies:
            c.start()

    def arrived(name, *copies):
        with jax.named_scope("wait_" + name):
            for c, _ in copies:
                c.wait_recv()

    def all_arrived(name, into, copy):
        with jax.named_scope("wait_" + name):
            pltpu.make_async_copy(into, into, rsem.at[copy[1]]).wait()

    with jax.named_scope("normalize_text"):
        load_t.wait()
        inv_t = inverse_norm(txt[...])
        tb[OWN0] = (txt[...] * inv_t).astype(BF)
    with jax.named_scope("barrier"):
        pl.semaphore_wait(barrier, len(others))

    t_p0 = copy_to(tb.at[OWN0, h0], tb.at[PAIR0, h0], pair)
    t_n = [copy_to(tb.at[OWN0, q], tb.at[NEAR0, q], near_to) for q in quarters]
    t_p1 = copy_to(tb.at[OWN0, h1], tb.at[PAIR0, h1], pair)
    s_own = copy_to(tb.at[OWN0], tb.at[OWN1], sibling)
    start(t_n[3], t_p0, t_n[2], t_p1, t_n[1], t_n[0], s_own)
    with jax.named_scope("normalize_image"):
        load_i.wait()
        inv_i = inverse_norm(img[...])
        ib[0] = (img[...] * inv_i).astype(BF)
    i_r0 = copy_to(ib.at[0, h0], ib.at[LEFT, h0], right)
    i_l1 = copy_to(ib.at[0, h1], ib.at[RIGHT, h1], left)
    i_r1 = copy_to(ib.at[0, h1], ib.at[LEFT, h1], right)
    i_l0 = copy_to(ib.at[0, h0], ib.at[RIGHT, h0], left)
    start(i_r0, i_l1, i_r1, i_l0)
    i_o0 = copy_to(ib.at[LEFT, h0], ib.at[OPP, h0], right)
    i_o1 = copy_to(ib.at[RIGHT, h1], ib.at[OPP, h1], left, i_o0)
    s_p0 = copy_to(tb.at[PAIR0, h0], tb.at[PAIR1, h0], sibling, s_own)
    s_n1 = copy_to(tb.at[NEAR0, h1], tb.at[NEAR1, h1], sibling)
    s_p1 = copy_to(tb.at[PAIR0, h1], tb.at[PAIR1, h1], sibling, s_own)
    s_n0 = copy_to(tb.at[NEAR0, h0], tb.at[NEAR1, h0], sibling, s_n1)
    s_f0 = copy_to(tb.at[FAR0, h0], tb.at[FAR1, h0], sibling)
    s_f1 = copy_to(tb.at[FAR0, h1], tb.at[FAR1, h1], sibling, s_f0)
    t_f0 = copy_to(tb.at[PAIR0, h0], tb.at[FAR0, h0], near_to)
    t_f1 = copy_to(tb.at[NEAR0, h1], tb.at[FAR0, h1], pair)
    t_q = [copy_to(tb.at[PAIR0, quarters[0]], tb.at[FAR0, quarters[0]], near_to, t_f0),
           copy_to(tb.at[NEAR0, quarters[1]], tb.at[FAR0, quarters[1]], pair),
           copy_to(tb.at[NEAR0, quarters[2]], tb.at[FAR0, quarters[2]], pair),
           copy_to(tb.at[NEAR0, quarters[3]], tb.at[FAR0, quarters[3]], pair, t_f1)]
    into_first = blk == n_blk - 1
    first = blk == 0

    load_s.wait()
    load_b.wait()
    temper = jnp.exp(jnp.full((1, 1), ls_ref[0], F32))
    offset = bi_ref[0]
    loss[...] = jnp.zeros_like(loss)

    def score(first, last, lo, hi):
        with jax.named_scope(f"score_{first}_{last}_{lo}_{hi}"):
            n, m = (last - first) * rows, (hi - lo) * rows
            dots = lax.dot_general(tb[first:last].reshape(n, width), ib[lo:hi].reshape(m, width),
                                   (((1,), (1,)), ((), ())), preferred_element_type=F32)
            logit = temper * dots + offset
            e = jnp.exp(-jnp.abs(logit))
            weight = jnp.where(logit >= 0, 1.0, e) * pl.reciprocal(1.0 + e, approx=True)
            signed = logit
            if first == OWN0 and lo == 0:
                r = lax.broadcasted_iota(jnp.int32, logit.shape, 0)
                paired = (r == lax.broadcasted_iota(jnp.int32, logit.shape, 1)) & (r < rows)
                weight = weight - paired.astype(F32)
                signed = jnp.where(paired, -logit, logit)
            coef[pl.ds(first * rows, n), pl.ds(lo * rows, m)] = (temper * weight).astype(BF)
            e = e.reshape(n // (8 * GROUP), GROUP, 8, m)
            p = e[:, 0]
            for g in range(1, GROUP):
                p = p + e[:, g] * (1.0 + p)
            log1p = jnp.where(p < 1e-3, p * (1.0 - 0.5 * p), jnp.log(1.0 + p))
            lost = (jnp.sum(jnp.maximum(signed, 0.0).reshape(n // 8, 8, m), axis=0)
                    + jnp.sum(log1p, axis=0))
            for slot in range(lo, hi):
                loss[slot] += lost[:, (slot - lo) * rows:(slot - lo + 1) * rows]

    def image_partial(lo, hi, first, last):
        return lax.dot_general(coef[first * rows:last * rows, lo * rows:hi * rows],
                               tb[first:last].reshape((last - first) * rows, width),
                               (((0,), (0,)), ((), ())), preferred_element_type=F32)

    back = [copy_to(sib_out.at[s], sib_in.at[s], sibling) for s in range(4)]
    f_p0 = copy_to(t_out.at[FAR - 1, h0], t_mid.at[0], pair)
    f_n1 = copy_to(t_out.at[FAR - 1, h1], t_mid.at[1], near_of)
    b_p0 = copy_to(t_out.at[PAIR - 1, h0], t_in.at[0, h0], pair)
    b_p1 = copy_to(t_out.at[PAIR - 1, h1], t_in.at[0, h1], pair, b_p0)
    b_n1 = copy_to(t_out.at[NEAR - 1, h1], t_in.at[1, h1], near_of, b_p0)
    b_n0 = copy_to(t_out.at[NEAR - 1, h0], t_in.at[1, h0], near_of, b_p0)
    f_r0 = copy_to(i_out.at[OPP - 1, h0], i_mid.at[0], right)
    f_l1 = copy_to(i_out.at[OPP - 1, h1], i_mid.at[1], left)
    b_r1 = copy_to(i_out.at[RIGHT - 1, h1], i_in.at[0, h1], right)
    b_r0 = copy_to(i_out.at[RIGHT - 1, h0], i_in.at[0, h0], right, b_r1)
    b_l0 = copy_to(i_out.at[LEFT - 1, h0], i_in.at[1, h0], left, b_r1)
    b_l1 = copy_to(i_out.at[LEFT - 1, h1], i_in.at[1, h1], left, b_r1)
    l_o = copy_to(loss.at[OPP], l_mid, right)
    l_r = copy_to(loss.at[RIGHT], l_in.at[0], right)
    l_l = copy_to(loss.at[LEFT], l_in.at[1], left, l_r)

    def text_partial(first, last):
        return jnp.dot(coef[first * rows:last * rows], ib[...].reshape(4 * rows, width),
                       preferred_element_type=F32)

    def to_sibling(s, part):
        sib_out[s] = part.astype(BF)
        start(back[s])

    def add_sibling(s, part):
        arrived(f"text_sibling_{s}", back[s])
        return part + sib_in[s].astype(F32)

    def pass_on(name, got, src, slot, part, middle, out):
        arrived(name, got)
        src[slot, part] = (src[slot, part].astype(F32) + middle[...].astype(F32)).astype(BF)
        start(out)

    def pass_loss():
        arrived("mid_loss", l_o)
        loss[RIGHT] += l_mid[...]
        start(l_r)

    def pass_right():
        pass_on("mid_r", f_r0, i_out, RIGHT - 1, h0, i_mid.at[0], b_r0)

    def pass_left():
        pass_on("mid_l", f_l1, i_out, LEFT - 1, h1, i_mid.at[1], b_l1)

    def pass_near():
        pass_on("mid_n", f_p0, t_out, NEAR - 1, h0, t_mid.at[0], b_n0)

    def pass_pair():
        pass_on("mid_p", f_n1, t_out, PAIR - 1, h1, t_mid.at[1], b_p1)

    assert len(landed) == N_LANDED
    puts = [pltpu.make_async_copy(held, out, lsem.at[i])
            for i, (held, out) in enumerate(((row, loss_hbm), (gi, gi_hbm), (gt, gt_hbm)))]

    def backnorm(values, inverse, grad):
        unit = values * inverse
        return inverse * (grad - unit * jnp.sum(unit * grad, axis=1, keepdims=True))

    def finish_loss():
        all_arrived("loss", l_in, l_r)
        total = loss[0] + l_in[0] + l_in[1]
        row[...] = jnp.sum(total, axis=0, keepdims=True) / mean
        puts[0].start()

    def finish_image():
        all_arrived("image_back", i_in, b_r1)
        with jax.named_scope("image_norm"):
            grad = gi[...] + i_in[0].astype(F32) + i_in[1].astype(F32)
            gi[...] = backnorm(img[...], inv_i, grad)
            puts[1].start()

    def finish_text():
        all_arrived("text_back", t_in, b_p0)
        with jax.named_scope("text_norm"):
            grad = gt[...] + t_in[0].astype(F32) + t_in[1].astype(F32)
            gt[...] = backnorm(txt[...], inv_t, grad)
            puts[2].start()

    def start_own_plane():
        arrived("first_p", t_p0)
        pl.when(into_first)(t_q[0][0].start)
        pl.when(jnp.logical_not(into_first))(t_f0[0].start)
        start(s_p0)
        arrived("first_i", i_r0, i_l1)
        start(i_o0)
        start(i_o1)

    @pl.when(jnp.logical_not(first))
    def _():
        start_own_plane()
        arrived("first_n", t_n[3], t_n[2])
        start(t_f1)
        start(s_n1)
        arrived("second_p", t_p1)
        start(s_p1)
        arrived("second_n", t_n[1], t_n[0])
        start(s_n0)
        arrived("second_i", i_r1, i_l0)
        score(OWN0, OWN1, 0, OPP)
        all_arrived("pair_sibling", tb.at[OWN1:NEAR0], s_own)
        score(OWN1, NEAR0, 0, OPP)
        all_arrived("near_sibling", tb.at[NEAR1], s_n1)
        score(NEAR0, FAR0, 0, OPP)
        arrived("far_t0", t_f0)
        start(s_f0)
        arrived("far_t1", t_f1)
        start(s_f1)
        all_arrived("opp_i", ib.at[OPP], i_o0)
        score(OWN0, FAR0, OPP, OPP + 1)
        score(FAR0, FAR1, 0, OPP + 1)
        all_arrived("far_sibling", tb.at[FAR1], s_f0)
        score(FAR1, FAR1 + 1, 0, OPP + 1)
        start(l_o)
        start(l_l)
        with jax.named_scope("text_far_1"):
            to_sibling(FAR, text_partial(FAR1, FAR1 + 1))
        with jax.named_scope("image_opp"):
            i_out[OPP - 1] = image_partial(OPP, OPP + 1, OWN0, FAR1 + 1).astype(BF)
            start(f_r0)
            start(f_l1)
        with jax.named_scope("text_far_0"):
            t_out[FAR - 1] = add_sibling(FAR, text_partial(FAR0, FAR1)).astype(BF)
            start(f_p0)
            start(f_n1)
        with jax.named_scope("text_mid"):
            mid = text_partial(OWN1, FAR0)
            to_sibling(PAIR, mid[rows:2 * rows])
            to_sibling(NEAR, mid[3 * rows:])
            to_sibling(OWN, mid[:rows])
            near = mid[2 * rows:3 * rows]
        with jax.named_scope("image_next"):
            part = image_partial(RIGHT, LEFT + 1, OWN0, FAR1 + 1)
            i_out[RIGHT - 1:LEFT] = part.astype(BF).reshape(2, rows, width)
            start(b_r1)
            start(b_l0)
        with jax.named_scope("text_near"):
            t_out[NEAR - 1] = add_sibling(NEAR, near).astype(BF)
            start(b_n1)
        with jax.named_scope("text_own"):
            own = text_partial(OWN0, OWN1)
            t_out[PAIR - 1] = add_sibling(PAIR, own[rows:]).astype(BF)
            start(b_p0)
            gt[...] = own[:rows]
        with jax.named_scope("image_own"):
            gi[...] = image_partial(0, 1, OWN0, FAR1 + 1)
        pass_loss()
        pass_right()
        pass_left()
        pass_near()
        pass_pair()
        gt[...] = add_sibling(OWN, gt[...])
        finish_loss()
        finish_image()
        finish_text()

    @pl.when(first)
    def _():
        start_own_plane()
        arrived("second_p", t_p1)
        start(s_p1)
        arrived("second_i", i_r1, i_l0)
        score(OWN0, OWN1, 0, OPP)
        all_arrived("pair_sibling", tb.at[OWN1:NEAR0], s_own)
        score(OWN1, NEAR0, 0, OPP)
        all_arrived("opp_i", ib.at[OPP], i_o0)
        score(OWN0, NEAR0, OPP, OPP + 1)
        arrived("first_n", t_n[3])
        start(t_q[3])
        arrived("second_n", t_n[2])
        start(t_q[2])
        start(s_n1)
        arrived("third_n", t_n[1])
        start(t_q[1])
        with jax.named_scope("text_block"):
            part = text_partial(OWN0, NEAR0)
            to_sibling(PAIR, part[3 * rows:])
            to_sibling(OWN, part[2 * rows:3 * rows])
            gt[...] = part[:rows]
            kept[...] = part[rows:2 * rows]
        arrived("last_n", t_n[0])
        start(s_n0)
        score(NEAR0, NEAR1, 0, OPP + 1)
        all_arrived("near_sibling", tb.at[NEAR1], s_n1)
        score(NEAR1, FAR0, 0, OPP + 1)
        arrived("far_t1", t_q[3], t_q[2])
        start(s_f1)
        arrived("far_t0", t_q[0], t_q[1])
        start(s_f0)
        score(FAR0, FAR1, 0, OPP + 1)
        with jax.named_scope("image_ahead"):
            gi[...] = image_partial(OPP, OPP + 1, OWN0, FAR0)
        t_out[PAIR - 1] = add_sibling(PAIR, kept[...]).astype(BF)
        start(b_p0)
        all_arrived("far_sibling", tb.at[FAR1], s_f0)
        score(FAR1, FAR1 + 1, OPP, OPP + 1)
        with jax.named_scope("image_opp"):
            i_out[OPP - 1] = (gi[...] + image_partial(OPP, OPP + 1, FAR0, FAR1 + 1)).astype(BF)
            start(f_r0)
            start(f_l1)
        score(FAR1, FAR1 + 1, 0, OPP)
        start(l_o)
        start(l_l)
        with jax.named_scope("text_far"):
            part = text_partial(NEAR0, FAR1 + 1)
            to_sibling(FAR, part[3 * rows:])
            to_sibling(NEAR, part[rows:2 * rows])
            kept[...] = part[2 * rows:3 * rows]
            near = part[:rows]
        with jax.named_scope("image_next"):
            part = image_partial(RIGHT, OPP, OWN0, FAR1 + 1)
            i_out[RIGHT - 1:LEFT] = part.astype(BF).reshape(2, rows, width)
            start(b_r1)
            start(b_l0)
        t_out[FAR - 1] = add_sibling(FAR, kept[...]).astype(BF)
        start(f_p0)
        start(f_n1)
        t_out[NEAR - 1] = add_sibling(NEAR, near).astype(BF)
        start(b_n1)
        pass_pair()
        gt[...] = add_sibling(OWN, gt[...])
        with jax.named_scope("image_own"):
            gi[...] = image_partial(0, 1, OWN0, FAR1 + 1)
        pass_loss()
        pass_right()
        pass_left()
        pass_near()
        finish_loss()
        finish_text()
        finish_image()

    with jax.named_scope("sends_end"):
        some = [t_f0[0], t_f1[0]] + [c for c, _ in t_q]
        for c in sent:
            if not any(c is o for o in some):
                c.wait_send()
        pl.when(into_first)(t_q[0][0].wait_send)
        pl.when(jnp.logical_not(into_first))(t_f0[0].wait_send)
        pl.when(jnp.logical_not(first))(t_f1[0].wait_send)
        for c, _ in t_q[1:]:
            pl.when(first)(c.wait_send)
    with jax.named_scope("put"):
        for c in puts:
            c.wait()


def hand_on(row, gi, gt, row_out, gi_out, gt_out, row_held, gi_held, gt_held, in_sem, out_sem):
    parts = [(row, row_held, row_out)]
    size = gi.shape[0] // PARTS
    for at in range(0, gi.shape[0], size):
        for src, held, out in ((gi, gi_held, gi_out), (gt, gt_held, gt_out)):
            parts.append(tuple(ref.at[pl.ds(at, size)] for ref in (src, held, out)))
    reads = [pltpu.make_async_copy(src, held, in_sem.at[i]) for i, (src, held, _) in enumerate(parts)]
    writes = [pltpu.make_async_copy(held, out, out_sem.at[i]) for i, (_, held, out) in enumerate(parts)]
    for c in reads:
        c.start()
    for r, w in zip(reads, writes):
        r.wait()
        w.start()
    for c in writes:
        c.wait()


def body(images, texts, log_scale, bias):
    rows, width = images.shape
    n_blk = lax.axis_size("blk")
    mean = STEPS * rows * lax.axis_size("grp")
    low = functools.partial(pltpu.VMEM, dtype=BF)
    full = functools.partial(pltpu.VMEM, dtype=F32)
    anywhere = pl.BlockSpec(memory_space=pl.ANY)
    results = (
        jax.ShapeDtypeStruct((1, rows), F32),
        jax.ShapeDtypeStruct((rows, width), F32),
        jax.ShapeDtypeStruct((rows, width), F32),
    )
    held = pl.pallas_call(
        functools.partial(kernel, n_blk, mean),
        out_shape=results,
        in_specs=[anywhere] * 4,
        out_specs=(anywhere,) * 3,
        scratch_shapes=[
            pltpu.SMEM((1,), F32), pltpu.SMEM((1,), F32),
            full((rows, width)), full((rows, width)),
            full((rows, width)), full((rows, width)), full((1, rows)),
            full((rows, width)),
            low((4, rows, width)),
            low((8, rows, width)),
            low((8 * rows, 4 * rows)),
            full((4, 8, rows)),
            low((4, rows, width)), low((4, rows, width)),
            low((3, rows, width)), low((2, rows // 2, width)), low((2, rows, width)),
            low((3, rows, width)), low((2, rows // 2, width)), low((2, rows, width)),
            full((8, rows)), full((2, 8, rows)),
            pltpu.SemaphoreType.DMA((4,)),
            pltpu.SemaphoreType.DMA((1,)),
            pltpu.SemaphoreType.DMA((N_LANDED,)),
        ],
        compiler_params=pltpu.CompilerParams(
            collective_id=0, has_side_effects=True, vmem_limit_bytes=(64 << 20) - (1 << 19)),
        name="pair_loss",
    )(log_scale, bias, images, texts)
    row_loss, image_grad, text_grad = pl.pallas_call(
        hand_on,
        out_shape=results,
        in_specs=[anywhere] * 3,
        out_specs=(anywhere,) * 3,
        scratch_shapes=[
            full((1, rows)), full((rows, width)), full((rows, width)),
            pltpu.SemaphoreType.DMA((2 * PARTS + 1,)), pltpu.SemaphoreType.DMA((2 * PARTS + 1,)),
        ],
        name="hand_on",
    )(*held)
    return row_loss.reshape(rows), image_grad, text_grad


def solution(mesh):
    in_specs = (P(("blk", "grp"), None), P(("blk", "grp"), None), P(), P())
    out_specs = (P(("blk", "grp")), P(("blk", "grp"), None), P(("blk", "grp"), None))
    return jax.shard_map(body, mesh=mesh, in_specs=in_specs, out_specs=out_specs, check_vma=False)
```

```python
import functools

import jax
import jax.numpy as jnp
from jax import lax
from jax.experimental import pallas as pl
from jax.experimental.pallas import tpu as pltpu
from jax.sharding import PartitionSpec as P

STEPS = 2
MESH = pl.DeviceIdType.MESH
BF = jnp.bfloat16
F32 = jnp.float32
N_LANDED = 30
GROUP = 16
PARTS = 4

OWN0, PAIR0, OWN1, PAIR1, NEAR0, NEAR1, FAR0, FAR1 = range(8)
OWN, PAIR, NEAR, FAR = range(4)
RIGHT, LEFT, OPP = 1, 2, 3


def places(n_blk):
    b = lax.axis_index("blk")
    g = lax.axis_index("grp")
    core = lax.rem(g, 2)
    x_lo = lax.rem(g // 2, 2)
    y = g // 4
    nxt = lax.rem(b + 1, n_blk)
    prv = lax.rem(b + n_blk - 1, n_blk)

    def member(yy, xx, kk):
        return (yy * 2 + xx) * 2 + kk

    sibling = (b, member(y, x_lo, 1 - core))
    pair = (b, member(y, 1 - x_lo, core))
    near_to = (nxt, member(y, 1 - x_lo, core))
    near_of = (prv, member(y, 1 - x_lo, core))
    right = (b, member(lax.rem(y + 1, 4), x_lo, core))
    left = (b, member(lax.rem(y + 3, 4), x_lo, core))
    return sibling, pair, near_to, near_of, right, left


def inverse_norm(values):
    return lax.rsqrt(jnp.sum(values * values, axis=1, keepdims=True) + 1e-06)


def kernel(n_blk, mean, ls_hbm, bi_hbm, img_hbm, txt_hbm, loss_hbm, gi_hbm, gt_hbm,
           ls_ref, bi_ref, img, txt, gi, gt, row, kept, ib, tb, coef, loss, sib_out, sib_in,
           t_out, t_mid, t_in, i_out, i_mid, i_in, l_mid, l_in, lsem, ssem, rsem):
    rows, width = img.shape
    half = rows // 2
    h0, h1 = pl.ds(0, half), pl.ds(half, half)
    quarters = [pl.ds(at, half // 2) for at in range(0, rows, half // 2)]
    blk = lax.axis_index("blk")
    sibling, pair, near_to, near_of, right, left = places(n_blk)
    barrier = pltpu.get_barrier_semaphore()
    others = [sibling, pair, near_of, right, left]
    for other in others:
        pl.semaphore_signal(barrier, inc=1, device_id=other, device_id_type=MESH)

    load_t = pltpu.make_async_copy(txt_hbm, txt, lsem.at[0])
    load_i = pltpu.make_async_copy(img_hbm, img, lsem.at[1])
    load_t.start()
    load_i.start()
    load_s = pltpu.make_async_copy(ls_hbm, ls_ref, lsem.at[2])
    load_b = pltpu.make_async_copy(bi_hbm, bi_ref, lsem.at[3])
    load_s.start()
    load_b.start()

    sent, landed = [], []

    def copy_to(src, dst, to, with_=None):
        if with_ is None:
            landed.append(None)
        slot = len(landed) - 1 if with_ is None else with_[1]
        copy = pltpu.make_async_remote_copy(
            src_ref=src, dst_ref=dst, send_sem=ssem.at[0], recv_sem=rsem.at[slot],
            device_id=to, device_id_type=MESH)
        sent.append(copy)
        return copy, slot

    def start(*copies):
        for c, _ in copies:
            c.start()

    def arrived(name, *copies):
        with jax.named_scope("wait_" + name):
            for c, _ in copies:
                c.wait_recv()

    def all_arrived(name, into, copy):
        with jax.named_scope("wait_" + name):
            pltpu.make_async_copy(into, into, rsem.at[copy[1]]).wait()

    with jax.named_scope("normalize_text"):
        load_t.wait()
        inv_t = inverse_norm(txt[...])
        tb[OWN0] = (txt[...] * inv_t).astype(BF)
    with jax.named_scope("barrier"):
        pl.semaphore_wait(barrier, len(others))

    t_p0 = copy_to(tb.at[OWN0, h0], tb.at[PAIR0, h0], pair)
    t_n = [copy_to(tb.at[OWN0, q], tb.at[NEAR0, q], near_to) for q in quarters]
    t_p1 = copy_to(tb.at[OWN0, h1], tb.at[PAIR0, h1], pair)
    s_own = copy_to(tb.at[OWN0], tb.at[OWN1], sibling)
    start(t_n[3], t_p0, t_n[2], t_p1, t_n[1], t_n[0], s_own)
    with jax.named_scope("normalize_image"):
        load_i.wait()
        inv_i = inverse_norm(img[...])
        ib[0] = (img[...] * inv_i).astype(BF)
    i_r0 = copy_to(ib.at[0, h0], ib.at[LEFT, h0], right)
    i_l1 = copy_to(ib.at[0, h1], ib.at[RIGHT, h1], left)
    i_r1 = copy_to(ib.at[0, h1], ib.at[LEFT, h1], right)
    i_l0 = copy_to(ib.at[0, h0], ib.at[RIGHT, h0], left)
    start(i_r0, i_l1, i_r1, i_l0)
    i_o0 = copy_to(ib.at[LEFT, h0], ib.at[OPP, h0], right)
    i_o1 = copy_to(ib.at[RIGHT, h1], ib.at[OPP, h1], left, i_o0)
    s_p0 = copy_to(tb.at[PAIR0, h0], tb.at[PAIR1, h0], sibling, s_own)
    s_n1 = copy_to(tb.at[NEAR0, h1], tb.at[NEAR1, h1], sibling)
    s_p1 = copy_to(tb.at[PAIR0, h1], tb.at[PAIR1, h1], sibling, s_own)
    s_n0 = copy_to(tb.at[NEAR0, h0], tb.at[NEAR1, h0], sibling, s_n1)
    s_f0 = copy_to(tb.at[FAR0, h0], tb.at[FAR1, h0], sibling)
    s_f1 = copy_to(tb.at[FAR0, h1], tb.at[FAR1, h1], sibling, s_f0)
    t_f0 = copy_to(tb.at[PAIR0, h0], tb.at[FAR0, h0], near_to)
    t_f1 = copy_to(tb.at[NEAR0, h1], tb.at[FAR0, h1], pair)
    t_q = [copy_to(tb.at[PAIR0, quarters[0]], tb.at[FAR0, quarters[0]], near_to, t_f0),
           copy_to(tb.at[NEAR0, quarters[1]], tb.at[FAR0, quarters[1]], pair),
           copy_to(tb.at[NEAR0, quarters[2]], tb.at[FAR0, quarters[2]], pair),
           copy_to(tb.at[NEAR0, quarters[3]], tb.at[FAR0, quarters[3]], pair, t_f1)]
    into_first = blk == n_blk - 1
    first = blk == 0

    load_s.wait()
    load_b.wait()
    temper = jnp.exp(jnp.full((1, 1), ls_ref[0], F32))
    offset = bi_ref[0]
    loss[...] = jnp.zeros_like(loss)

    def score(first, last, lo, hi):
        with jax.named_scope(f"score_{first}_{last}_{lo}_{hi}"):
            n, m = (last - first) * rows, (hi - lo) * rows
            dots = lax.dot_general(tb[first:last].reshape(n, width), ib[lo:hi].reshape(m, width),
                                   (((1,), (1,)), ((), ())), preferred_element_type=F32)
            logit = temper * dots + offset
            e = jnp.exp(-jnp.abs(logit))
            weight = jnp.where(logit >= 0, 1.0, e) * pl.reciprocal(1.0 + e, approx=True)
            signed = logit
            if first == OWN0 and lo == 0:
                r = lax.broadcasted_iota(jnp.int32, logit.shape, 0)
                paired = (r == lax.broadcasted_iota(jnp.int32, logit.shape, 1)) & (r < rows)
                weight = weight - paired.astype(F32)
                signed = jnp.where(paired, -logit, logit)
            coef[pl.ds(first * rows, n), pl.ds(lo * rows, m)] = (temper * weight).astype(BF)
            e = e.reshape(n // (8 * GROUP), GROUP, 8, m)
            p = e[:, 0]
            for g in range(1, GROUP):
                p = p + e[:, g] * (1.0 + p)
            log1p = jnp.where(p < 1e-3, p * (1.0 - 0.5 * p), jnp.log(1.0 + p))
            lost = (jnp.sum(jnp.maximum(signed, 0.0).reshape(n // 8, 8, m), axis=0)
                    + jnp.sum(log1p, axis=0))
            for slot in range(lo, hi):
                loss[slot] += lost[:, (slot - lo) * rows:(slot - lo + 1) * rows]

    def image_partial(lo, hi, first, last):
        return lax.dot_general(coef[first * rows:last * rows, lo * rows:hi * rows],
                               tb[first:last].reshape((last - first) * rows, width),
                               (((0,), (0,)), ((), ())), preferred_element_type=F32)

    back = [copy_to(sib_out.at[s], sib_in.at[s], sibling) for s in range(4)]
    f_p0 = copy_to(t_out.at[FAR - 1, h0], t_mid.at[0], pair)
    f_n1 = copy_to(t_out.at[FAR - 1, h1], t_mid.at[1], near_of)
    b_p0 = copy_to(t_out.at[PAIR - 1, h0], t_in.at[0, h0], pair)
    b_p1 = copy_to(t_out.at[PAIR - 1, h1], t_in.at[0, h1], pair, b_p0)
    b_n1 = copy_to(t_out.at[NEAR - 1, h1], t_in.at[1, h1], near_of, b_p0)
    b_n0 = copy_to(t_out.at[NEAR - 1, h0], t_in.at[1, h0], near_of, b_p0)
    f_r0 = copy_to(i_out.at[OPP - 1, h0], i_mid.at[0], right)
    f_l1 = copy_to(i_out.at[OPP - 1, h1], i_mid.at[1], left)
    b_r1 = copy_to(i_out.at[RIGHT - 1, h1], i_in.at[0, h1], right)
    b_r0 = copy_to(i_out.at[RIGHT - 1, h0], i_in.at[0, h0], right, b_r1)
    b_l0 = copy_to(i_out.at[LEFT - 1, h0], i_in.at[1, h0], left, b_r1)
    b_l1 = copy_to(i_out.at[LEFT - 1, h1], i_in.at[1, h1], left, b_r1)
    l_o = copy_to(loss.at[OPP], l_mid, right)
    l_r = copy_to(loss.at[RIGHT], l_in.at[0], right)
    l_l = copy_to(loss.at[LEFT], l_in.at[1], left, l_r)

    def text_partial(first, last):
        return jnp.dot(coef[first * rows:last * rows], ib[...].reshape(4 * rows, width),
                       preferred_element_type=F32)

    def to_sibling(s, part):
        sib_out[s] = part.astype(BF)
        start(back[s])

    def add_sibling(s, part):
        arrived(f"text_sibling_{s}", back[s])
        return part + sib_in[s].astype(F32)

    def pass_on(name, got, src, slot, part, middle, out):
        arrived(name, got)
        src[slot, part] = (src[slot, part].astype(F32) + middle[...].astype(F32)).astype(BF)
        start(out)

    def pass_loss():
        arrived("mid_loss", l_o)
        loss[RIGHT] += l_mid[...]
        start(l_r)

    def pass_right():
        pass_on("mid_r", f_r0, i_out, RIGHT - 1, h0, i_mid.at[0], b_r0)

    def pass_left():
        pass_on("mid_l", f_l1, i_out, LEFT - 1, h1, i_mid.at[1], b_l1)

    def pass_near():
        pass_on("mid_n", f_p0, t_out, NEAR - 1, h0, t_mid.at[0], b_n0)

    def pass_pair():
        pass_on("mid_p", f_n1, t_out, PAIR - 1, h1, t_mid.at[1], b_p1)

    assert len(landed) == N_LANDED
    puts = [pltpu.make_async_copy(held, out, lsem.at[i])
            for i, (held, out) in enumerate(((row, loss_hbm), (gt, gt_hbm), (gi.at[h0], gi_hbm.at[h0]),
                                             (gi.at[h1], gi_hbm.at[h1])))]

    def backnorm(values, inverse, grad):
        unit = values * inverse
        return inverse * (grad - unit * jnp.sum(unit * grad, axis=1, keepdims=True))

    def finish_loss():
        all_arrived("loss", l_in, l_r)
        total = loss[0] + l_in[0] + l_in[1]
        row[...] = jnp.sum(total, axis=0, keepdims=True) / mean
        puts[0].start()

    def finish_image():
        all_arrived("image_back", i_in, b_r1)
        with jax.named_scope("image_norm"):
            for at, put in ((0, puts[2]), (half, puts[3])):
                part = pl.ds(at, half)
                grad = gi[part] + i_in[0, part].astype(F32) + i_in[1, part].astype(F32)
                gi[part] = backnorm(img[part], inv_i[at:at + half], grad)
                put.start()

    def finish_text():
        all_arrived("text_back", t_in, b_p0)
        with jax.named_scope("text_norm"):
            grad = gt[...] + t_in[0].astype(F32) + t_in[1].astype(F32)
            gt[...] = backnorm(txt[...], inv_t, grad)
            puts[1].start()

    def start_own_plane():
        arrived("first_p", t_p0)
        pl.when(into_first)(t_q[0][0].start)
        pl.when(jnp.logical_not(into_first))(t_f0[0].start)
        start(s_p0)
        arrived("first_i", i_r0, i_l1)
        start(i_o0)
        start(i_o1)

    @pl.when(jnp.logical_not(first))
    def _():
        start_own_plane()
        arrived("first_n", t_n[3], t_n[2])
        start(t_f1)
        start(s_n1)
        arrived("second_p", t_p1)
        start(s_p1)
        arrived("second_n", t_n[1], t_n[0])
        start(s_n0)
        arrived("second_i", i_r1, i_l0)
        score(OWN0, OWN1, 0, OPP)
        all_arrived("pair_sibling", tb.at[OWN1:NEAR0], s_own)
        score(OWN1, NEAR0, 0, OPP)
        all_arrived("near_sibling", tb.at[NEAR1], s_n1)
        score(NEAR0, FAR0, 0, OPP)
        arrived("far_t0", t_f0)
        start(s_f0)
        arrived("far_t1", t_f1)
        start(s_f1)
        all_arrived("opp_i", ib.at[OPP], i_o0)
        score(OWN0, FAR0, OPP, OPP + 1)
        score(FAR0, FAR1, 0, OPP + 1)
        all_arrived("far_sibling", tb.at[FAR1], s_f0)
        score(FAR1, FAR1 + 1, 0, OPP + 1)
        start(l_o)
        start(l_l)
        with jax.named_scope("text_far_1"):
            to_sibling(FAR, text_partial(FAR1, FAR1 + 1))
        with jax.named_scope("image_opp"):
            i_out[OPP - 1] = image_partial(OPP, OPP + 1, OWN0, FAR1 + 1).astype(BF)
            start(f_r0)
            start(f_l1)
        with jax.named_scope("text_far_0"):
            t_out[FAR - 1] = add_sibling(FAR, text_partial(FAR0, FAR1)).astype(BF)
            start(f_p0)
            start(f_n1)
        with jax.named_scope("text_mid"):
            mid = text_partial(OWN1, FAR0)
            to_sibling(PAIR, mid[rows:2 * rows])
            to_sibling(NEAR, mid[3 * rows:])
            to_sibling(OWN, mid[:rows])
            near = mid[2 * rows:3 * rows]
        with jax.named_scope("image_next"):
            part = image_partial(RIGHT, LEFT + 1, OWN0, FAR1 + 1)
            i_out[RIGHT - 1:LEFT] = part.astype(BF).reshape(2, rows, width)
            start(b_r1)
            start(b_l0)
        with jax.named_scope("text_near"):
            t_out[NEAR - 1] = add_sibling(NEAR, near).astype(BF)
            start(b_n1)
        with jax.named_scope("text_own"):
            own = text_partial(OWN0, OWN1)
            t_out[PAIR - 1] = add_sibling(PAIR, own[rows:]).astype(BF)
            start(b_p0)
            gt[...] = own[:rows]
        with jax.named_scope("image_own"):
            gi[...] = image_partial(0, 1, OWN0, FAR1 + 1)
        pass_loss()
        pass_right()
        pass_left()
        pass_near()
        pass_pair()
        gt[...] = add_sibling(OWN, gt[...])
        finish_loss()
        finish_image()
        finish_text()

    @pl.when(first)
    def _():
        start_own_plane()
        arrived("second_p", t_p1)
        start(s_p1)
        arrived("second_i", i_r1, i_l0)
        score(OWN0, OWN1, 0, OPP)
        all_arrived("pair_sibling", tb.at[OWN1:NEAR0], s_own)
        score(OWN1, NEAR0, 0, OPP)
        all_arrived("opp_i", ib.at[OPP], i_o0)
        score(OWN0, NEAR0, OPP, OPP + 1)
        arrived("first_n", t_n[3])
        start(t_q[3])
        arrived("second_n", t_n[2])
        start(t_q[2], s_n1)
        with jax.named_scope("text_block"):
            part = text_partial(OWN0, NEAR0)
            to_sibling(PAIR, part[3 * rows:])
            to_sibling(OWN, part[2 * rows:3 * rows])
            gt[...] = part[:rows]
            kept[...] = part[rows:2 * rows]
        arrived("third_n", t_n[1])
        start(t_q[1])
        arrived("last_n", t_n[0])
        start(s_n0)
        score(NEAR0, NEAR1, 0, OPP + 1)
        all_arrived("near_sibling", tb.at[NEAR1], s_n1)
        score(NEAR1, FAR0, 0, OPP + 1)
        arrived("far_t1", t_q[3], t_q[2])
        start(s_f1)
        arrived("far_t0", t_q[0], t_q[1])
        start(s_f0)
        score(FAR0, FAR1, 0, OPP + 1)
        with jax.named_scope("image_ahead"):
            gi[...] = image_partial(OPP, OPP + 1, OWN0, FAR0)
        all_arrived("far_sibling", tb.at[FAR1], s_f0)
        score(FAR1, FAR1 + 1, OPP, OPP + 1)
        with jax.named_scope("image_opp"):
            i_out[OPP - 1] = (gi[...] + image_partial(OPP, OPP + 1, FAR0, FAR1 + 1)).astype(BF)
            start(f_r0, f_l1)
        t_out[PAIR - 1] = add_sibling(PAIR, kept[...]).astype(BF)
        start(b_p0)
        score(FAR1, FAR1 + 1, 0, OPP)
        start(l_o, l_l)
        with jax.named_scope("text_far_1"):
            to_sibling(FAR, text_partial(FAR1, FAR1 + 1))
        with jax.named_scope("image_next"):
            part = image_partial(RIGHT, OPP, OWN0, FAR1 + 1)
            i_out[RIGHT - 1:LEFT] = part.astype(BF).reshape(2, rows, width)
            start(b_r1, b_l0)
        with jax.named_scope("text_far_0"):
            t_out[FAR - 1] = add_sibling(FAR, text_partial(FAR0, FAR1)).astype(BF)
            start(f_p0, f_n1)
        with jax.named_scope("text_near"):
            near = text_partial(NEAR0, FAR0)
            to_sibling(NEAR, near[rows:])
        pass_pair()
        gt[...] = add_sibling(OWN, gt[...])
        t_out[NEAR - 1] = add_sibling(NEAR, near[:rows]).astype(BF)
        start(b_n1)
        with jax.named_scope("image_own"):
            gi[...] = image_partial(0, 1, OWN0, FAR1 + 1)
        pass_loss()
        pass_right()
        pass_left()
        pass_near()
        finish_loss()
        finish_text()
        finish_image()

    with jax.named_scope("sends_end"):
        some = [t_f0[0], t_f1[0]] + [c for c, _ in t_q]
        for c in sent:
            if not any(c is o for o in some):
                c.wait_send()
        pl.when(into_first)(t_q[0][0].wait_send)
        pl.when(jnp.logical_not(into_first))(t_f0[0].wait_send)
        pl.when(jnp.logical_not(first))(t_f1[0].wait_send)
        for c, _ in t_q[1:]:
            pl.when(first)(c.wait_send)
    with jax.named_scope("put"):
        for c in puts:
            c.wait()


def hand_on(row, gi, gt, row_out, gi_out, gt_out, row_held, gi_held, gt_held, in_sem, out_sem):
    parts = [(row, row_held, row_out)]
    size = gi.shape[0] // PARTS
    for at in range(0, gi.shape[0], size):
        for src, held, out in ((gi, gi_held, gi_out), (gt, gt_held, gt_out)):
            parts.append(tuple(ref.at[pl.ds(at, size)] for ref in (src, held, out)))
    reads = [pltpu.make_async_copy(src, held, in_sem.at[i]) for i, (src, held, _) in enumerate(parts)]
    writes = [pltpu.make_async_copy(held, out, out_sem.at[i]) for i, (_, held, out) in enumerate(parts)]
    for c in reads:
        c.start()
    for r, w in zip(reads, writes):
        r.wait()
        w.start()
    for c in writes:
        c.wait()


def body(images, texts, log_scale, bias):
    rows, width = images.shape
    n_blk = lax.axis_size("blk")
    mean = STEPS * rows * lax.axis_size("grp")
    low = functools.partial(pltpu.VMEM, dtype=BF)
    full = functools.partial(pltpu.VMEM, dtype=F32)
    anywhere = pl.BlockSpec(memory_space=pl.ANY)
    results = (
        jax.ShapeDtypeStruct((1, rows), F32),
        jax.ShapeDtypeStruct((rows, width), F32),
        jax.ShapeDtypeStruct((rows, width), F32),
    )
    held = pl.pallas_call(
        functools.partial(kernel, n_blk, mean),
        out_shape=results,
        in_specs=[anywhere] * 4,
        out_specs=(anywhere,) * 3,
        scratch_shapes=[
            pltpu.SMEM((1,), F32), pltpu.SMEM((1,), F32),
            full((rows, width)), full((rows, width)),
            full((rows, width)), full((rows, width)), full((1, rows)),
            full((rows, width)),
            low((4, rows, width)),
            low((8, rows, width)),
            low((8 * rows, 4 * rows)),
            full((4, 8, rows)),
            low((4, rows, width)), low((4, rows, width)),
            low((3, rows, width)), low((2, rows // 2, width)), low((2, rows, width)),
            low((3, rows, width)), low((2, rows // 2, width)), low((2, rows, width)),
            full((8, rows)), full((2, 8, rows)),
            pltpu.SemaphoreType.DMA((4,)),
            pltpu.SemaphoreType.DMA((1,)),
            pltpu.SemaphoreType.DMA((N_LANDED,)),
        ],
        compiler_params=pltpu.CompilerParams(
            collective_id=0, has_side_effects=True, vmem_limit_bytes=(64 << 20) - (1 << 19)),
        name="pair_loss",
    )(log_scale, bias, images, texts)
    row_loss, image_grad, text_grad = pl.pallas_call(
        hand_on,
        out_shape=results,
        in_specs=[anywhere] * 3,
        out_specs=(anywhere,) * 3,
        scratch_shapes=[
            full((1, rows)), full((rows, width)), full((rows, width)),
            pltpu.SemaphoreType.DMA((2 * PARTS + 1,)), pltpu.SemaphoreType.DMA((2 * PARTS + 1,)),
        ],
        name="hand_on",
    )(*held)
    return row_loss.reshape(rows), image_grad, text_grad


def solution(mesh):
    in_specs = (P(("blk", "grp"), None), P(("blk", "grp"), None), P(), P())
    out_specs = (P(("blk", "grp")), P(("blk", "grp"), None), P(("blk", "grp"), None))
    return jax.shard_map(body, mesh=mesh, in_specs=in_specs, out_specs=out_specs, check_vma=False)
```

```python
import functools

import jax
import jax.numpy as jnp
from jax import lax
from jax.experimental import pallas as pl
from jax.experimental.pallas import tpu as pltpu
from jax.sharding import PartitionSpec as P

STEPS = 2
MESH = pl.DeviceIdType.MESH
BF = jnp.bfloat16
F32 = jnp.float32
N_LANDED = 30
GROUP = 16
PARTS = 4

OWN0, PAIR0, OWN1, PAIR1, NEAR0, NEAR1, FAR0, FAR1 = range(8)
OWN, PAIR, NEAR, FAR = range(4)
RIGHT, LEFT, OPP = 1, 2, 3


def places(n_blk):
    b = lax.axis_index("blk")
    g = lax.axis_index("grp")
    core = lax.rem(g, 2)
    x_lo = lax.rem(g // 2, 2)
    y = g // 4
    nxt = lax.rem(b + 1, n_blk)
    prv = lax.rem(b + n_blk - 1, n_blk)

    def member(yy, xx, kk):
        return (yy * 2 + xx) * 2 + kk

    sibling = (b, member(y, x_lo, 1 - core))
    pair = (b, member(y, 1 - x_lo, core))
    near_to = (nxt, member(y, 1 - x_lo, core))
    near_of = (prv, member(y, 1 - x_lo, core))
    right = (b, member(lax.rem(y + 1, 4), x_lo, core))
    left = (b, member(lax.rem(y + 3, 4), x_lo, core))
    return sibling, pair, near_to, near_of, right, left


def inverse_norm(values):
    return lax.rsqrt(jnp.sum(values * values, axis=1, keepdims=True) + 1e-06)


def kernel(n_blk, mean, ls_hbm, bi_hbm, img_hbm, txt_hbm, loss_hbm, gi_hbm, gt_hbm,
           ls_ref, bi_ref, img, txt, gi, gt, row, kept, ib, tb, coef, loss, sib_out, sib_in,
           t_out, t_mid, t_in, i_out, i_mid, i_in, l_mid, l_in, lsem, ssem, rsem):
    rows, width = img.shape
    half = rows // 2
    h0, h1 = pl.ds(0, half), pl.ds(half, half)
    quarters = [pl.ds(at, half // 2) for at in range(0, rows, half // 2)]
    blk = lax.axis_index("blk")
    sibling, pair, near_to, near_of, right, left = places(n_blk)
    barrier = pltpu.get_barrier_semaphore()
    others = [sibling, pair, near_of, right, left]
    for other in others:
        pl.semaphore_signal(barrier, inc=1, device_id=other, device_id_type=MESH)

    load_t = pltpu.make_async_copy(txt_hbm, txt, lsem.at[0])
    load_i = pltpu.make_async_copy(img_hbm, img, lsem.at[1])
    load_t.start()
    load_i.start()
    load_s = pltpu.make_async_copy(ls_hbm, ls_ref, lsem.at[2])
    load_b = pltpu.make_async_copy(bi_hbm, bi_ref, lsem.at[3])
    load_s.start()
    load_b.start()

    sent, landed = [], []

    def copy_to(src, dst, to, with_=None):
        if with_ is None:
            landed.append(None)
        slot = len(landed) - 1 if with_ is None else with_[1]
        copy = pltpu.make_async_remote_copy(
            src_ref=src, dst_ref=dst, send_sem=ssem.at[0], recv_sem=rsem.at[slot],
            device_id=to, device_id_type=MESH)
        sent.append(copy)
        return copy, slot

    def start(*copies):
        for c, _ in copies:
            c.start()

    def arrived(name, *copies):
        with jax.named_scope("wait_" + name):
            for c, _ in copies:
                c.wait_recv()

    def all_arrived(name, into, copy):
        with jax.named_scope("wait_" + name):
            pltpu.make_async_copy(into, into, rsem.at[copy[1]]).wait()

    with jax.named_scope("normalize_text"):
        load_t.wait()
        inv_t = inverse_norm(txt[...])
        tb[OWN0] = (txt[...] * inv_t).astype(BF)
    with jax.named_scope("barrier"):
        pl.semaphore_wait(barrier, len(others))

    t_p0 = copy_to(tb.at[OWN0, h0], tb.at[PAIR0, h0], pair)
    t_n = [copy_to(tb.at[OWN0, q], tb.at[NEAR0, q], near_to) for q in quarters]
    t_p1 = copy_to(tb.at[OWN0, h1], tb.at[PAIR0, h1], pair)
    s_own = copy_to(tb.at[OWN0], tb.at[OWN1], sibling)
    start(t_n[3], t_p0, t_n[2], t_p1, t_n[1], t_n[0], s_own)
    with jax.named_scope("normalize_image"):
        load_i.wait()
        inv_i = inverse_norm(img[...])
        ib[0] = (img[...] * inv_i).astype(BF)
    i_r0 = copy_to(ib.at[0, h0], ib.at[LEFT, h0], right)
    i_l1 = copy_to(ib.at[0, h1], ib.at[RIGHT, h1], left)
    i_r1 = copy_to(ib.at[0, h1], ib.at[LEFT, h1], right)
    i_l0 = copy_to(ib.at[0, h0], ib.at[RIGHT, h0], left)
    start(i_r0, i_l1, i_r1, i_l0)
    i_o0 = copy_to(ib.at[LEFT, h0], ib.at[OPP, h0], right)
    i_o1 = copy_to(ib.at[RIGHT, h1], ib.at[OPP, h1], left, i_o0)
    s_p0 = copy_to(tb.at[PAIR0, h0], tb.at[PAIR1, h0], sibling, s_own)
    s_n1 = copy_to(tb.at[NEAR0, h1], tb.at[NEAR1, h1], sibling)
    s_p1 = copy_to(tb.at[PAIR0, h1], tb.at[PAIR1, h1], sibling, s_own)
    s_n0 = copy_to(tb.at[NEAR0, h0], tb.at[NEAR1, h0], sibling, s_n1)
    s_f0 = copy_to(tb.at[FAR0, h0], tb.at[FAR1, h0], sibling)
    s_f1 = copy_to(tb.at[FAR0, h1], tb.at[FAR1, h1], sibling, s_f0)
    t_f0 = copy_to(tb.at[PAIR0, h0], tb.at[FAR0, h0], near_to)
    t_f1 = copy_to(tb.at[NEAR0, h1], tb.at[FAR0, h1], pair)
    t_q = [copy_to(tb.at[PAIR0, quarters[0]], tb.at[FAR0, quarters[0]], near_to, t_f0),
           copy_to(tb.at[NEAR0, quarters[1]], tb.at[FAR0, quarters[1]], pair),
           copy_to(tb.at[NEAR0, quarters[2]], tb.at[FAR0, quarters[2]], pair),
           copy_to(tb.at[NEAR0, quarters[3]], tb.at[FAR0, quarters[3]], pair, t_f1)]
    into_first = blk == n_blk - 1
    first = blk == 0

    load_s.wait()
    load_b.wait()
    temper = jnp.exp(jnp.full((1, 1), ls_ref[0], F32))
    offset = bi_ref[0]
    loss[...] = jnp.zeros_like(loss)

    def score(first, last, lo, hi):
        with jax.named_scope(f"score_{first}_{last}_{lo}_{hi}"):
            n, m = (last - first) * rows, (hi - lo) * rows
            dots = lax.dot_general(tb[first:last].reshape(n, width), ib[lo:hi].reshape(m, width),
                                   (((1,), (1,)), ((), ())), preferred_element_type=F32)
            logit = temper * dots + offset
            e = jnp.exp(-jnp.abs(logit))
            signed, paired = logit, None
            if first == OWN0 and lo == 0:
                r = lax.broadcasted_iota(jnp.int32, logit.shape, 0)
                paired = (r == lax.broadcasted_iota(jnp.int32, logit.shape, 1)) & (r < rows)
                signed = jnp.where(paired, -logit, logit)
            weight = jnp.where(signed >= 0, 1.0, e) * pl.reciprocal(1.0 + e, approx=True)
            if paired is not None:
                weight = jnp.where(paired, -weight, weight)
            coef[pl.ds(first * rows, n), pl.ds(lo * rows, m)] = (temper * weight).astype(BF)
            e = e.reshape(n // (8 * GROUP), GROUP, 8, m)
            p = e[:, 0]
            for g in range(1, GROUP):
                p = p + e[:, g] * (1.0 + p)
            log1p = jnp.where(p < 1e-3, p * (1.0 - 0.5 * p), jnp.log(1.0 + p))
            lost = (jnp.sum(jnp.maximum(signed, 0.0).reshape(n // 8, 8, m), axis=0)
                    + jnp.sum(log1p, axis=0))
            for slot in range(lo, hi):
                loss[slot] += lost[:, (slot - lo) * rows:(slot - lo + 1) * rows]

    def image_partial(lo, hi, first, last):
        return lax.dot_general(coef[first * rows:last * rows, lo * rows:hi * rows],
                               tb[first:last].reshape((last - first) * rows, width),
                               (((0,), (0,)), ((), ())), preferred_element_type=F32)

    back = [copy_to(sib_out.at[s], sib_in.at[s], sibling) for s in range(4)]
    f_p0 = copy_to(t_out.at[FAR - 1, h0], t_mid.at[0], pair)
    f_n1 = copy_to(t_out.at[FAR - 1, h1], t_mid.at[1], near_of)
    b_p0 = copy_to(t_out.at[PAIR - 1, h0], t_in.at[0, h0], pair)
    b_p1 = copy_to(t_out.at[PAIR - 1, h1], t_in.at[0, h1], pair, b_p0)
    b_n1 = copy_to(t_out.at[NEAR - 1, h1], t_in.at[1, h1], near_of, b_p0)
    b_n0 = copy_to(t_out.at[NEAR - 1, h0], t_in.at[1, h0], near_of, b_p0)
    f_r0 = copy_to(i_out.at[OPP - 1, h0], i_mid.at[0], right)
    f_l1 = copy_to(i_out.at[OPP - 1, h1], i_mid.at[1], left)
    b_r1 = copy_to(i_out.at[RIGHT - 1, h1], i_in.at[0, h1], right)
    b_r0 = copy_to(i_out.at[RIGHT - 1, h0], i_in.at[0, h0], right, b_r1)
    b_l0 = copy_to(i_out.at[LEFT - 1, h0], i_in.at[1, h0], left, b_r1)
    b_l1 = copy_to(i_out.at[LEFT - 1, h1], i_in.at[1, h1], left, b_r1)
    l_o = copy_to(loss.at[OPP], l_mid, right)
    l_r = copy_to(loss.at[RIGHT], l_in.at[0], right)
    l_l = copy_to(loss.at[LEFT], l_in.at[1], left, l_r)

    def text_partial(first, last):
        return jnp.dot(coef[first * rows:last * rows], ib[...].reshape(4 * rows, width),
                       preferred_element_type=F32)

    def to_sibling(s, part):
        sib_out[s] = part.astype(BF)
        start(back[s])

    def add_sibling(s, part):
        arrived(f"text_sibling_{s}", back[s])
        return part + sib_in[s].astype(F32)

    def pass_on(name, got, src, slot, part, middle, out):
        arrived(name, got)
        src[slot, part] = (src[slot, part].astype(F32) + middle[...].astype(F32)).astype(BF)
        start(out)

    def pass_loss():
        arrived("mid_loss", l_o)
        loss[RIGHT] += l_mid[...]
        start(l_r)

    def pass_right():
        pass_on("mid_r", f_r0, i_out, RIGHT - 1, h0, i_mid.at[0], b_r0)

    def pass_left():
        pass_on("mid_l", f_l1, i_out, LEFT - 1, h1, i_mid.at[1], b_l1)

    def pass_near():
        pass_on("mid_n", f_p0, t_out, NEAR - 1, h0, t_mid.at[0], b_n0)

    def pass_pair():
        pass_on("mid_p", f_n1, t_out, PAIR - 1, h1, t_mid.at[1], b_p1)

    assert len(landed) == N_LANDED
    puts = [pltpu.make_async_copy(held, out, lsem.at[i])
            for i, (held, out) in enumerate(((row, loss_hbm), (gt, gt_hbm), (gi.at[h0], gi_hbm.at[h0]),
                                             (gi.at[h1], gi_hbm.at[h1])))]

    def backnorm(values, inverse, grad):
        unit = values * inverse
        return inverse * (grad - unit * jnp.sum(unit * grad, axis=1, keepdims=True))

    def finish_loss():
        all_arrived("loss", l_in, l_r)
        total = loss[0] + l_in[0] + l_in[1]
        row[...] = jnp.sum(total, axis=0, keepdims=True) / mean
        puts[0].start()

    def finish_image():
        all_arrived("image_back", i_in, b_r1)
        with jax.named_scope("image_norm"):
            for at, put in ((0, puts[2]), (half, puts[3])):
                part = pl.ds(at, half)
                grad = gi[part] + i_in[0, part].astype(F32) + i_in[1, part].astype(F32)
                gi[part] = backnorm(img[part], inv_i[at:at + half], grad)
                put.start()

    def finish_text():
        all_arrived("text_back", t_in, b_p0)
        with jax.named_scope("text_norm"):
            grad = gt[...] + t_in[0].astype(F32) + t_in[1].astype(F32)
            gt[...] = backnorm(txt[...], inv_t, grad)
            puts[1].start()

    def start_own_plane():
        arrived("first_p", t_p0)
        pl.when(into_first)(t_q[0][0].start)
        pl.when(jnp.logical_not(into_first))(t_f0[0].start)
        start(s_p0)
        arrived("first_i", i_r0, i_l1)
        start(i_o0)
        start(i_o1)

    @pl.when(jnp.logical_not(first))
    def _():
        start_own_plane()
        arrived("first_n", t_n[3], t_n[2])
        start(t_f1)
        start(s_n1)
        arrived("second_p", t_p1)
        start(s_p1)
        arrived("second_n", t_n[1], t_n[0])
        start(s_n0)
        arrived("second_i", i_r1, i_l0)
        score(OWN0, OWN1, 0, OPP)
        all_arrived("pair_sibling", tb.at[OWN1:NEAR0], s_own)
        score(OWN1, NEAR0, 0, OPP)
        all_arrived("near_sibling", tb.at[NEAR1], s_n1)
        score(NEAR0, FAR0, 0, OPP)
        arrived("far_t0", t_f0)
        start(s_f0)
        arrived("far_t1", t_f1)
        start(s_f1)
        all_arrived("opp_i", ib.at[OPP], i_o0)
        score(OWN0, FAR0, OPP, OPP + 1)
        score(FAR0, FAR1, 0, OPP + 1)
        all_arrived("far_sibling", tb.at[FAR1], s_f0)
        score(FAR1, FAR1 + 1, 0, OPP + 1)
        start(l_o)
        start(l_l)
        with jax.named_scope("text_far_1"):
            to_sibling(FAR, text_partial(FAR1, FAR1 + 1))
        with jax.named_scope("image_opp"):
            i_out[OPP - 1] = image_partial(OPP, OPP + 1, OWN0, FAR1 + 1).astype(BF)
            start(f_r0)
            start(f_l1)
        with jax.named_scope("text_far_0"):
            t_out[FAR - 1] = add_sibling(FAR, text_partial(FAR0, FAR1)).astype(BF)
            start(f_p0)
            start(f_n1)
        with jax.named_scope("text_mid"):
            mid = text_partial(OWN1, FAR0)
            to_sibling(PAIR, mid[rows:2 * rows])
            to_sibling(NEAR, mid[3 * rows:])
            to_sibling(OWN, mid[:rows])
            near = mid[2 * rows:3 * rows]
        with jax.named_scope("image_next"):
            part = image_partial(RIGHT, LEFT + 1, OWN0, FAR1 + 1)
            i_out[RIGHT - 1:LEFT] = part.astype(BF).reshape(2, rows, width)
            start(b_r1)
            start(b_l0)
        with jax.named_scope("text_near"):
            t_out[NEAR - 1] = add_sibling(NEAR, near).astype(BF)
            start(b_n1)
        with jax.named_scope("text_own"):
            own = text_partial(OWN0, OWN1)
            t_out[PAIR - 1] = add_sibling(PAIR, own[rows:]).astype(BF)
            start(b_p0)
            gt[...] = own[:rows]
        with jax.named_scope("image_own"):
            gi[...] = image_partial(0, 1, OWN0, FAR1 + 1)
        pass_loss()
        pass_right()
        pass_left()
        pass_near()
        pass_pair()
        gt[...] = add_sibling(OWN, gt[...])
        finish_loss()
        finish_image()
        finish_text()

    @pl.when(first)
    def _():
        start_own_plane()
        arrived("second_p", t_p1)
        start(s_p1)
        arrived("second_i", i_r1, i_l0)
        score(OWN0, OWN1, 0, OPP)
        all_arrived("pair_sibling", tb.at[OWN1:NEAR0], s_own)
        score(OWN1, NEAR0, 0, OPP)
        all_arrived("opp_i", ib.at[OPP], i_o0)
        score(OWN0, NEAR0, OPP, OPP + 1)
        arrived("first_n", t_n[3])
        start(t_q[3])
        arrived("second_n", t_n[2])
        start(t_q[2], s_n1)
        with jax.named_scope("text_block"):
            part = text_partial(OWN0, NEAR0)
            to_sibling(PAIR, part[3 * rows:])
            to_sibling(OWN, part[2 * rows:3 * rows])
            gt[...] = part[:rows]
            kept[...] = part[rows:2 * rows]
        arrived("third_n", t_n[1])
        start(t_q[1])
        arrived("last_n", t_n[0])
        start(s_n0)
        score(NEAR0, NEAR1, 0, OPP + 1)
        all_arrived("near_sibling", tb.at[NEAR1], s_n1)
        score(NEAR1, FAR0, 0, OPP + 1)
        arrived("far_t1", t_q[3], t_q[2])
        start(s_f1)
        arrived("far_t0", t_q[0], t_q[1])
        start(s_f0)
        score(FAR0, FAR1, 0, OPP + 1)
        with jax.named_scope("image_ahead"):
            gi[...] = image_partial(OPP, OPP + 1, OWN0, FAR0)
        all_arrived("far_sibling", tb.at[FAR1], s_f0)
        score(FAR1, FAR1 + 1, OPP, OPP + 1)
        with jax.named_scope("image_opp"):
            i_out[OPP - 1] = (gi[...] + image_partial(OPP, OPP + 1, FAR0, FAR1 + 1)).astype(BF)
            start(f_r0, f_l1)
        t_out[PAIR - 1] = add_sibling(PAIR, kept[...]).astype(BF)
        start(b_p0)
        score(FAR1, FAR1 + 1, 0, OPP)
        start(l_o, l_l)
        with jax.named_scope("text_far_1"):
            to_sibling(FAR, text_partial(FAR1, FAR1 + 1))
        with jax.named_scope("image_next"):
            part = image_partial(RIGHT, OPP, OWN0, FAR1 + 1)
            i_out[RIGHT - 1:LEFT] = part.astype(BF).reshape(2, rows, width)
            start(b_r1, b_l0)
        with jax.named_scope("text_far_0"):
            t_out[FAR - 1] = add_sibling(FAR, text_partial(FAR0, FAR1)).astype(BF)
            start(f_p0, f_n1)
        with jax.named_scope("text_near"):
            near = text_partial(NEAR0, FAR0)
            to_sibling(NEAR, near[rows:])
        pass_pair()
        gt[...] = add_sibling(OWN, gt[...])
        t_out[NEAR - 1] = add_sibling(NEAR, near[:rows]).astype(BF)
        start(b_n1)
        with jax.named_scope("image_own"):
            gi[...] = image_partial(0, 1, OWN0, FAR1 + 1)
        pass_loss()
        pass_right()
        pass_left()
        pass_near()
        finish_loss()
        finish_text()
        finish_image()

    with jax.named_scope("sends_end"):
        some = [t_f0[0], t_f1[0]] + [c for c, _ in t_q]
        for c in sent:
            if not any(c is o for o in some):
                c.wait_send()
        pl.when(into_first)(t_q[0][0].wait_send)
        pl.when(jnp.logical_not(into_first))(t_f0[0].wait_send)
        pl.when(jnp.logical_not(first))(t_f1[0].wait_send)
        for c, _ in t_q[1:]:
            pl.when(first)(c.wait_send)
    with jax.named_scope("put"):
        for c in puts:
            c.wait()


def hand_on(row, gi, gt, row_out, gi_out, gt_out, row_held, gi_held, gt_held, in_sem, out_sem):
    parts = [(row, row_held, row_out)]
    size = gi.shape[0] // PARTS
    for at in range(0, gi.shape[0], size):
        for src, held, out in ((gi, gi_held, gi_out), (gt, gt_held, gt_out)):
            parts.append(tuple(ref.at[pl.ds(at, size)] for ref in (src, held, out)))
    reads = [pltpu.make_async_copy(src, held, in_sem.at[i]) for i, (src, held, _) in enumerate(parts)]
    writes = [pltpu.make_async_copy(held, out, out_sem.at[i]) for i, (_, held, out) in enumerate(parts)]
    for c in reads:
        c.start()
    for r, w in zip(reads, writes):
        r.wait()
        w.start()
    for c in writes:
        c.wait()


def body(images, texts, log_scale, bias):
    rows, width = images.shape
    n_blk = lax.axis_size("blk")
    mean = STEPS * rows * lax.axis_size("grp")
    low = functools.partial(pltpu.VMEM, dtype=BF)
    full = functools.partial(pltpu.VMEM, dtype=F32)
    anywhere = pl.BlockSpec(memory_space=pl.ANY)
    results = (
        jax.ShapeDtypeStruct((1, rows), F32),
        jax.ShapeDtypeStruct((rows, width), F32),
        jax.ShapeDtypeStruct((rows, width), F32),
    )
    held = pl.pallas_call(
        functools.partial(kernel, n_blk, mean),
        out_shape=results,
        in_specs=[anywhere] * 4,
        out_specs=(anywhere,) * 3,
        scratch_shapes=[
            pltpu.SMEM((1,), F32), pltpu.SMEM((1,), F32),
            full((rows, width)), full((rows, width)),
            full((rows, width)), full((rows, width)), full((1, rows)),
            full((rows, width)),
            low((4, rows, width)),
            low((8, rows, width)),
            low((8 * rows, 4 * rows)),
            full((4, 8, rows)),
            low((4, rows, width)), low((4, rows, width)),
            low((3, rows, width)), low((2, rows // 2, width)), low((2, rows, width)),
            low((3, rows, width)), low((2, rows // 2, width)), low((2, rows, width)),
            full((8, rows)), full((2, 8, rows)),
            pltpu.SemaphoreType.DMA((4,)),
            pltpu.SemaphoreType.DMA((1,)),
            pltpu.SemaphoreType.DMA((N_LANDED,)),
        ],
        compiler_params=pltpu.CompilerParams(
            collective_id=0, has_side_effects=True, vmem_limit_bytes=(64 << 20) - (1 << 19)),
        name="pair_loss",
    )(log_scale, bias, images, texts)
    row_loss, image_grad, text_grad = pl.pallas_call(
        hand_on,
        out_shape=results,
        in_specs=[anywhere] * 3,
        out_specs=(anywhere,) * 3,
        scratch_shapes=[
            full((1, rows)), full((rows, width)), full((rows, width)),
            pltpu.SemaphoreType.DMA((2 * PARTS + 1,)), pltpu.SemaphoreType.DMA((2 * PARTS + 1,)),
        ],
        name="hand_on",
    )(*held)
    return row_loss.reshape(rows), image_grad, text_grad


def solution(mesh):
    in_specs = (P(("blk", "grp"), None), P(("blk", "grp"), None), P(), P())
    out_specs = (P(("blk", "grp")), P(("blk", "grp"), None), P(("blk", "grp"), None))
    return jax.shard_map(body, mesh=mesh, in_specs=in_specs, out_specs=out_specs, check_vma=False)
```

```python
import functools

import jax
import jax.numpy as jnp
from jax import lax
from jax.experimental import pallas as pl
from jax.experimental.pallas import tpu as pltpu
from jax.sharding import PartitionSpec as P

STEPS = 2
MESH = pl.DeviceIdType.MESH
BF = jnp.bfloat16
F32 = jnp.float32
N_LANDED = 30
GROUP = 16
PARTS = 4

OWN0, PAIR0, OWN1, PAIR1, NEAR0, NEAR1, FAR0, FAR1 = range(8)
OWN, PAIR, NEAR, FAR = range(4)
RIGHT, LEFT, OPP = 1, 2, 3


def places(n_blk):
    b = lax.axis_index("blk")
    g = lax.axis_index("grp")
    core = lax.rem(g, 2)
    x_lo = lax.rem(g // 2, 2)
    y = g // 4
    nxt = lax.rem(b + 1, n_blk)
    prv = lax.rem(b + n_blk - 1, n_blk)

    def member(yy, xx, kk):
        return (yy * 2 + xx) * 2 + kk

    sibling = (b, member(y, x_lo, 1 - core))
    pair = (b, member(y, 1 - x_lo, core))
    near_to = (nxt, member(y, 1 - x_lo, core))
    near_of = (prv, member(y, 1 - x_lo, core))
    right = (b, member(lax.rem(y + 1, 4), x_lo, core))
    left = (b, member(lax.rem(y + 3, 4), x_lo, core))
    return sibling, pair, near_to, near_of, right, left


def inverse_norm(values):
    return lax.rsqrt(jnp.sum(values * values, axis=1, keepdims=True) + 1e-06)


def kernel(n_blk, mean, ls_hbm, bi_hbm, img_hbm, txt_hbm, loss_hbm, gi_hbm, gt_hbm,
           ls_ref, bi_ref, img, txt, gi, gt, row, kept, ib, tb, coef, loss, sib_out, sib_in,
           t_out, t_mid, t_in, i_out, i_mid, i_in, l_mid, l_in, lsem, ssem, rsem):
    rows, width = img.shape
    half = rows // 2
    h0, h1 = pl.ds(0, half), pl.ds(half, half)
    quarters = [pl.ds(at, half // 2) for at in range(0, rows, half // 2)]
    blk = lax.axis_index("blk")
    sibling, pair, near_to, near_of, right, left = places(n_blk)
    barrier = pltpu.get_barrier_semaphore()
    others = [sibling, pair, near_of, right, left]
    for other in others:
        pl.semaphore_signal(barrier, inc=1, device_id=other, device_id_type=MESH)

    load_t = pltpu.make_async_copy(txt_hbm, txt, lsem.at[0])
    load_i = pltpu.make_async_copy(img_hbm, img, lsem.at[1])
    load_t.start()
    load_i.start()
    load_s = pltpu.make_async_copy(ls_hbm, ls_ref, lsem.at[2])
    load_b = pltpu.make_async_copy(bi_hbm, bi_ref, lsem.at[3])
    load_s.start()
    load_b.start()

    sent, landed = [], []

    def copy_to(src, dst, to, with_=None):
        if with_ is None:
            landed.append(None)
        slot = len(landed) - 1 if with_ is None else with_[1]
        copy = pltpu.make_async_remote_copy(
            src_ref=src, dst_ref=dst, send_sem=ssem.at[0], recv_sem=rsem.at[slot],
            device_id=to, device_id_type=MESH)
        sent.append(copy)
        return copy, slot

    def start(*copies):
        for c, _ in copies:
            c.start()

    def arrived(name, *copies):
        with jax.named_scope("wait_" + name):
            for c, _ in copies:
                c.wait_recv()

    def all_arrived(name, into, copy):
        with jax.named_scope("wait_" + name):
            pltpu.make_async_copy(into, into, rsem.at[copy[1]]).wait()

    with jax.named_scope("normalize_text"):
        load_t.wait()
        inv_t = inverse_norm(txt[...])
        tb[OWN0] = (txt[...] * inv_t).astype(BF)
    with jax.named_scope("barrier"):
        pl.semaphore_wait(barrier, len(others))

    t_p0 = copy_to(tb.at[OWN0, h0], tb.at[PAIR0, h0], pair)
    t_n = [copy_to(tb.at[OWN0, q], tb.at[NEAR0, q], near_to) for q in quarters]
    t_p1 = copy_to(tb.at[OWN0, h1], tb.at[PAIR0, h1], pair)
    s_own = copy_to(tb.at[OWN0], tb.at[OWN1], sibling)
    start(t_n[3], t_p0, t_n[2], t_p1, t_n[1], t_n[0], s_own)
    with jax.named_scope("normalize_image"):
        load_i.wait()
        inv_i = inverse_norm(img[...])
        ib[0] = (img[...] * inv_i).astype(BF)
    i_r0 = copy_to(ib.at[0, h0], ib.at[LEFT, h0], right)
    i_l1 = copy_to(ib.at[0, h1], ib.at[RIGHT, h1], left)
    i_r1 = copy_to(ib.at[0, h1], ib.at[LEFT, h1], right)
    i_l0 = copy_to(ib.at[0, h0], ib.at[RIGHT, h0], left)
    start(i_r0, i_l1, i_r1, i_l0)
    i_o0 = copy_to(ib.at[LEFT, h0], ib.at[OPP, h0], right)
    i_o1 = copy_to(ib.at[RIGHT, h1], ib.at[OPP, h1], left, i_o0)
    s_p0 = copy_to(tb.at[PAIR0, h0], tb.at[PAIR1, h0], sibling, s_own)
    s_n1 = copy_to(tb.at[NEAR0, h1], tb.at[NEAR1, h1], sibling)
    s_p1 = copy_to(tb.at[PAIR0, h1], tb.at[PAIR1, h1], sibling, s_own)
    s_n0 = copy_to(tb.at[NEAR0, h0], tb.at[NEAR1, h0], sibling, s_n1)
    s_f0 = copy_to(tb.at[FAR0, h0], tb.at[FAR1, h0], sibling)
    s_f1 = copy_to(tb.at[FAR0, h1], tb.at[FAR1, h1], sibling, s_f0)
    t_f0 = copy_to(tb.at[PAIR0, h0], tb.at[FAR0, h0], near_to)
    t_f1 = copy_to(tb.at[NEAR0, h1], tb.at[FAR0, h1], pair)
    t_q = [copy_to(tb.at[PAIR0, quarters[0]], tb.at[FAR0, quarters[0]], near_to, t_f0),
           copy_to(tb.at[NEAR0, quarters[1]], tb.at[FAR0, quarters[1]], pair),
           copy_to(tb.at[NEAR0, quarters[2]], tb.at[FAR0, quarters[2]], pair),
           copy_to(tb.at[NEAR0, quarters[3]], tb.at[FAR0, quarters[3]], pair, t_f1)]
    into_first = blk == n_blk - 1
    first = blk == 0

    load_s.wait()
    load_b.wait()
    temper = jnp.exp(jnp.full((1, 1), ls_ref[0], F32))
    offset = bi_ref[0]
    loss[...] = jnp.zeros_like(loss)

    def score(first, last, lo, hi, weights=True, losses=True):
        with jax.named_scope(f"score_{first}_{last}_{lo}_{hi}"):
            n, m = (last - first) * rows, (hi - lo) * rows
            dots = lax.dot_general(tb[first:last].reshape(n, width), ib[lo:hi].reshape(m, width),
                                   (((1,), (1,)), ((), ())), preferred_element_type=F32)
            logit = temper * dots + offset
            e = jnp.exp(-jnp.abs(logit))
            signed, paired = logit, None
            if first == OWN0 and lo == 0:
                r = lax.broadcasted_iota(jnp.int32, logit.shape, 0)
                paired = (r == lax.broadcasted_iota(jnp.int32, logit.shape, 1)) & (r < rows)
                signed = jnp.where(paired, -logit, logit)
            if weights:
                weight = jnp.where(signed >= 0, 1.0, e) * pl.reciprocal(1.0 + e, approx=True)
                if paired is not None:
                    weight = jnp.where(paired, -weight, weight)
                coef[pl.ds(first * rows, n), pl.ds(lo * rows, m)] = (temper * weight).astype(BF)
            if not losses:
                return
            e = e.reshape(n // (8 * GROUP), GROUP, 8, m)
            p = e[:, 0]
            for g in range(1, GROUP):
                p = p + e[:, g] * (1.0 + p)
            log1p = jnp.where(p < 1e-3, p * (1.0 - 0.5 * p), jnp.log(1.0 + p))
            lost = (jnp.sum(jnp.maximum(signed, 0.0).reshape(n // 8, 8, m), axis=0)
                    + jnp.sum(log1p, axis=0))
            for slot in range(lo, hi):
                loss[slot] += lost[:, (slot - lo) * rows:(slot - lo + 1) * rows]

    def image_partial(lo, hi, first, last):
        return lax.dot_general(coef[first * rows:last * rows, lo * rows:hi * rows],
                               tb[first:last].reshape((last - first) * rows, width),
                               (((0,), (0,)), ((), ())), preferred_element_type=F32)

    back = [copy_to(sib_out.at[s], sib_in.at[s], sibling) for s in range(4)]
    f_p0 = copy_to(t_out.at[FAR - 1, h0], t_mid.at[0], pair)
    f_n1 = copy_to(t_out.at[FAR - 1, h1], t_mid.at[1], near_of)
    b_p0 = copy_to(t_out.at[PAIR - 1, h0], t_in.at[0, h0], pair)
    b_p1 = copy_to(t_out.at[PAIR - 1, h1], t_in.at[0, h1], pair, b_p0)
    b_n1 = copy_to(t_out.at[NEAR - 1, h1], t_in.at[1, h1], near_of, b_p0)
    b_n0 = copy_to(t_out.at[NEAR - 1, h0], t_in.at[1, h0], near_of, b_p0)
    f_r0 = copy_to(i_out.at[OPP - 1, h0], i_mid.at[0], right)
    f_l1 = copy_to(i_out.at[OPP - 1, h1], i_mid.at[1], left)
    b_r1 = copy_to(i_out.at[RIGHT - 1, h1], i_in.at[0, h1], right)
    b_r0 = copy_to(i_out.at[RIGHT - 1, h0], i_in.at[0, h0], right, b_r1)
    b_l0 = copy_to(i_out.at[LEFT - 1, h0], i_in.at[1, h0], left, b_r1)
    b_l1 = copy_to(i_out.at[LEFT - 1, h1], i_in.at[1, h1], left, b_r1)
    l_o = copy_to(loss.at[OPP], l_mid, right)
    l_r = copy_to(loss.at[RIGHT], l_in.at[0], right)
    l_l = copy_to(loss.at[LEFT], l_in.at[1], left, l_r)

    def text_partial(first, last):
        return jnp.dot(coef[first * rows:last * rows], ib[...].reshape(4 * rows, width),
                       preferred_element_type=F32)

    def to_sibling(s, part):
        sib_out[s] = part.astype(BF)
        start(back[s])

    def add_sibling(s, part):
        arrived(f"text_sibling_{s}", back[s])
        return part + sib_in[s].astype(F32)

    def pass_on(name, got, src, slot, part, middle, out):
        arrived(name, got)
        src[slot, part] = (src[slot, part].astype(F32) + middle[...].astype(F32)).astype(BF)
        start(out)

    def pass_loss():
        arrived("mid_loss", l_o)
        loss[RIGHT] += l_mid[...]
        start(l_r)

    def pass_right():
        pass_on("mid_r", f_r0, i_out, RIGHT - 1, h0, i_mid.at[0], b_r0)

    def pass_left():
        pass_on("mid_l", f_l1, i_out, LEFT - 1, h1, i_mid.at[1], b_l1)

    def pass_near():
        pass_on("mid_n", f_p0, t_out, NEAR - 1, h0, t_mid.at[0], b_n0)

    def pass_pair():
        pass_on("mid_p", f_n1, t_out, PAIR - 1, h1, t_mid.at[1], b_p1)

    assert len(landed) == N_LANDED
    puts = [pltpu.make_async_copy(held, out, lsem.at[i])
            for i, (held, out) in enumerate(((row, loss_hbm), (gt, gt_hbm), (gi.at[h0], gi_hbm.at[h0]),
                                             (gi.at[h1], gi_hbm.at[h1])))]

    def backnorm(values, inverse, grad):
        unit = values * inverse
        return inverse * (grad - unit * jnp.sum(unit * grad, axis=1, keepdims=True))

    def finish_loss():
        all_arrived("loss", l_in, l_r)
        total = loss[0] + l_in[0] + l_in[1]
        row[...] = jnp.sum(total, axis=0, keepdims=True) / mean
        puts[0].start()

    def finish_image():
        all_arrived("image_back", i_in, b_r1)
        with jax.named_scope("image_norm"):
            for at, put in ((0, puts[2]), (half, puts[3])):
                part = pl.ds(at, half)
                grad = gi[part] + i_in[0, part].astype(F32) + i_in[1, part].astype(F32)
                gi[part] = backnorm(img[part], inv_i[at:at + half], grad)
                put.start()

    def finish_text():
        all_arrived("text_back", t_in, b_p0)
        with jax.named_scope("text_norm"):
            grad = gt[...] + t_in[0].astype(F32) + t_in[1].astype(F32)
            gt[...] = backnorm(txt[...], inv_t, grad)
            puts[1].start()

    def start_own_plane():
        arrived("first_p", t_p0)
        pl.when(into_first)(t_q[0][0].start)
        pl.when(jnp.logical_not(into_first))(t_f0[0].start)
        start(s_p0)
        arrived("first_i", i_r0, i_l1)
        start(i_o0)
        start(i_o1)

    @pl.when(jnp.logical_not(first))
    def _():
        start_own_plane()
        arrived("first_n", t_n[3], t_n[2])
        start(t_f1)
        start(s_n1)
        arrived("second_p", t_p1)
        start(s_p1)
        arrived("second_n", t_n[1], t_n[0])
        start(s_n0)
        arrived("second_i", i_r1, i_l0)
        score(OWN0, OWN1, 0, OPP)
        all_arrived("pair_sibling", tb.at[OWN1:NEAR0], s_own)
        score(OWN1, NEAR0, 0, OPP)
        all_arrived("near_sibling", tb.at[NEAR1], s_n1)
        score(NEAR0, FAR0, 0, OPP)
        arrived("far_t0", t_f0)
        start(s_f0)
        arrived("far_t1", t_f1)
        start(s_f1)
        all_arrived("opp_i", ib.at[OPP], i_o0)
        score(OWN0, FAR0, OPP, OPP + 1)
        score(FAR0, FAR1, 0, OPP + 1)
        all_arrived("far_sibling", tb.at[FAR1], s_f0)
        score(FAR1, FAR1 + 1, 0, OPP + 1)
        start(l_o)
        start(l_l)
        with jax.named_scope("text_far_1"):
            to_sibling(FAR, text_partial(FAR1, FAR1 + 1))
        with jax.named_scope("image_opp"):
            i_out[OPP - 1] = image_partial(OPP, OPP + 1, OWN0, FAR1 + 1).astype(BF)
            start(f_r0)
            start(f_l1)
        with jax.named_scope("text_far_0"):
            t_out[FAR - 1] = add_sibling(FAR, text_partial(FAR0, FAR1)).astype(BF)
            start(f_p0)
            start(f_n1)
        with jax.named_scope("text_mid"):
            mid = text_partial(OWN1, FAR0)
            to_sibling(PAIR, mid[rows:2 * rows])
            to_sibling(NEAR, mid[3 * rows:])
            to_sibling(OWN, mid[:rows])
            near = mid[2 * rows:3 * rows]
        with jax.named_scope("image_next"):
            part = image_partial(RIGHT, LEFT + 1, OWN0, FAR1 + 1)
            i_out[RIGHT - 1:LEFT] = part.astype(BF).reshape(2, rows, width)
            start(b_r1)
            start(b_l0)
        with jax.named_scope("text_near"):
            t_out[NEAR - 1] = add_sibling(NEAR, near).astype(BF)
            start(b_n1)
        with jax.named_scope("text_own"):
            own = text_partial(OWN0, OWN1)
            t_out[PAIR - 1] = add_sibling(PAIR, own[rows:]).astype(BF)
            start(b_p0)
            gt[...] = own[:rows]
        with jax.named_scope("image_own"):
            gi[...] = image_partial(0, 1, OWN0, FAR1 + 1)
        pass_loss()
        pass_right()
        pass_left()
        pass_near()
        pass_pair()
        gt[...] = add_sibling(OWN, gt[...])
        finish_loss()
        finish_image()
        finish_text()

    @pl.when(first)
    def _():
        start_own_plane()
        arrived("second_p", t_p1)
        start(s_p1)
        arrived("second_i", i_r1, i_l0)
        score(OWN0, OWN1, 0, OPP)
        all_arrived("pair_sibling", tb.at[OWN1:NEAR0], s_own)
        score(OWN1, NEAR0, 0, OPP)
        all_arrived("opp_i", ib.at[OPP], i_o0)
        score(OWN0, NEAR0, OPP, OPP + 1)
        arrived("first_n", t_n[3])
        start(t_q[3])
        arrived("second_n", t_n[2])
        start(t_q[2], s_n1)
        with jax.named_scope("text_block"):
            part = text_partial(OWN0, NEAR0)
            to_sibling(PAIR, part[3 * rows:])
            to_sibling(OWN, part[2 * rows:3 * rows])
            gt[...] = part[:rows]
            kept[...] = part[rows:2 * rows]
        arrived("third_n", t_n[1])
        start(t_q[1])
        arrived("last_n", t_n[0])
        start(s_n0)
        score(NEAR0, NEAR1, 0, OPP + 1)
        all_arrived("near_sibling", tb.at[NEAR1], s_n1)
        score(NEAR1, FAR0, 0, OPP + 1)
        arrived("far_t1", t_q[3], t_q[2])
        start(s_f1)
        arrived("far_t0", t_q[0], t_q[1])
        start(s_f0)
        score(FAR0, FAR1, 0, OPP + 1)
        with jax.named_scope("image_ahead"):
            gi[...] = image_partial(OPP, OPP + 1, OWN0, FAR0)
        all_arrived("far_sibling", tb.at[FAR1], s_f0)
        score(FAR1, FAR1 + 1, OPP, OPP + 1, losses=False)
        with jax.named_scope("image_opp"):
            i_out[OPP - 1] = (gi[...] + image_partial(OPP, OPP + 1, FAR0, FAR1 + 1)).astype(BF)
            start(f_r0, f_l1)
        t_out[PAIR - 1] = add_sibling(PAIR, kept[...]).astype(BF)
        start(b_p0)
        score(FAR1, FAR1 + 1, 0, OPP)
        score(FAR1, FAR1 + 1, OPP, OPP + 1, weights=False)
        start(l_o, l_l)
        with jax.named_scope("text_far_1"):
            to_sibling(FAR, text_partial(FAR1, FAR1 + 1))
        with jax.named_scope("image_next"):
            part = image_partial(RIGHT, OPP, OWN0, FAR1 + 1)
            i_out[RIGHT - 1:LEFT] = part.astype(BF).reshape(2, rows, width)
            start(b_r1, b_l0)
        with jax.named_scope("text_far_0"):
            t_out[FAR - 1] = add_sibling(FAR, text_partial(FAR0, FAR1)).astype(BF)
            start(f_p0, f_n1)
        with jax.named_scope("text_near"):
            near = text_partial(NEAR0, FAR0)
            to_sibling(NEAR, near[rows:])
        pass_pair()
        gt[...] = add_sibling(OWN, gt[...])
        t_out[NEAR - 1] = add_sibling(NEAR, near[:rows]).astype(BF)
        start(b_n1)
        with jax.named_scope("image_own"):
            gi[...] = image_partial(0, 1, OWN0, FAR1 + 1)
        pass_loss()
        pass_right()
        pass_left()
        pass_near()
        finish_loss()
        finish_text()
        finish_image()

    with jax.named_scope("sends_end"):
        some = [t_f0[0], t_f1[0]] + [c for c, _ in t_q]
        for c in sent:
            if not any(c is o for o in some):
                c.wait_send()
        pl.when(into_first)(t_q[0][0].wait_send)
        pl.when(jnp.logical_not(into_first))(t_f0[0].wait_send)
        pl.when(jnp.logical_not(first))(t_f1[0].wait_send)
        for c, _ in t_q[1:]:
            pl.when(first)(c.wait_send)
    with jax.named_scope("put"):
        for c in puts:
            c.wait()


def hand_on(row, gi, gt, row_out, gi_out, gt_out, row_held, gi_held, gt_held, in_sem, out_sem):
    parts = [(row, row_held, row_out)]
    size = gi.shape[0] // PARTS
    for at in range(0, gi.shape[0], size):
        for src, held, out in ((gi, gi_held, gi_out), (gt, gt_held, gt_out)):
            parts.append(tuple(ref.at[pl.ds(at, size)] for ref in (src, held, out)))
    reads = [pltpu.make_async_copy(src, held, in_sem.at[i]) for i, (src, held, _) in enumerate(parts)]
    writes = [pltpu.make_async_copy(held, out, out_sem.at[i]) for i, (_, held, out) in enumerate(parts)]
    for c in reads:
        c.start()
    for r, w in zip(reads, writes):
        r.wait()
        w.start()
    for c in writes:
        c.wait()


def body(images, texts, log_scale, bias):
    rows, width = images.shape
    n_blk = lax.axis_size("blk")
    mean = STEPS * rows * lax.axis_size("grp")
    low = functools.partial(pltpu.VMEM, dtype=BF)
    full = functools.partial(pltpu.VMEM, dtype=F32)
    anywhere = pl.BlockSpec(memory_space=pl.ANY)
    results = (
        jax.ShapeDtypeStruct((1, rows), F32),
        jax.ShapeDtypeStruct((rows, width), F32),
        jax.ShapeDtypeStruct((rows, width), F32),
    )
    held = pl.pallas_call(
        functools.partial(kernel, n_blk, mean),
        out_shape=results,
        in_specs=[anywhere] * 4,
        out_specs=(anywhere,) * 3,
        scratch_shapes=[
            pltpu.SMEM((1,), F32), pltpu.SMEM((1,), F32),
            full((rows, width)), full((rows, width)),
            full((rows, width)), full((rows, width)), full((1, rows)),
            full((rows, width)),
            low((4, rows, width)),
            low((8, rows, width)),
            low((8 * rows, 4 * rows)),
            full((4, 8, rows)),
            low((4, rows, width)), low((4, rows, width)),
            low((3, rows, width)), low((2, rows // 2, width)), low((2, rows, width)),
            low((3, rows, width)), low((2, rows // 2, width)), low((2, rows, width)),
            full((8, rows)), full((2, 8, rows)),
            pltpu.SemaphoreType.DMA((4,)),
            pltpu.SemaphoreType.DMA((1,)),
            pltpu.SemaphoreType.DMA((N_LANDED,)),
        ],
        compiler_params=pltpu.CompilerParams(
            collective_id=0, has_side_effects=True, vmem_limit_bytes=(64 << 20) - (1 << 19)),
        name="pair_loss",
    )(log_scale, bias, images, texts)
    row_loss, image_grad, text_grad = pl.pallas_call(
        hand_on,
        out_shape=results,
        in_specs=[anywhere] * 3,
        out_specs=(anywhere,) * 3,
        scratch_shapes=[
            full((1, rows)), full((rows, width)), full((rows, width)),
            pltpu.SemaphoreType.DMA((2 * PARTS + 1,)), pltpu.SemaphoreType.DMA((2 * PARTS + 1,)),
        ],
        name="hand_on",
    )(*held)
    return row_loss.reshape(rows), image_grad, text_grad


def solution(mesh):
    in_specs = (P(("blk", "grp"), None), P(("blk", "grp"), None), P(), P())
    out_specs = (P(("blk", "grp")), P(("blk", "grp"), None), P(("blk", "grp"), None))
    return jax.shard_map(body, mesh=mesh, in_specs=in_specs, out_specs=out_specs, check_vma=False)
```

```python
import functools

import jax
import jax.numpy as jnp
from jax import lax
from jax.experimental import pallas as pl
from jax.experimental.pallas import tpu as pltpu
from jax.sharding import PartitionSpec as P

STEPS = 2
MESH = pl.DeviceIdType.MESH
BF = jnp.bfloat16
F32 = jnp.float32
N_LANDED = 30
GROUP = 16
PARTS = 2

OWN0, PAIR0, OWN1, PAIR1, NEAR0, NEAR1, FAR0, FAR1 = range(8)
OWN, PAIR, NEAR, FAR = range(4)
RIGHT, LEFT, OPP = 1, 2, 3


def places(n_blk):
    b = lax.axis_index("blk")
    g = lax.axis_index("grp")
    core = lax.rem(g, 2)
    x_lo = lax.rem(g // 2, 2)
    y = g // 4
    nxt = lax.rem(b + 1, n_blk)
    prv = lax.rem(b + n_blk - 1, n_blk)

    def member(yy, xx, kk):
        return (yy * 2 + xx) * 2 + kk

    sibling = (b, member(y, x_lo, 1 - core))
    pair = (b, member(y, 1 - x_lo, core))
    near_to = (nxt, member(y, 1 - x_lo, core))
    near_of = (prv, member(y, 1 - x_lo, core))
    right = (b, member(lax.rem(y + 1, 4), x_lo, core))
    left = (b, member(lax.rem(y + 3, 4), x_lo, core))
    return sibling, pair, near_to, near_of, right, left


def inverse_norm(values):
    return lax.rsqrt(jnp.sum(values * values, axis=1, keepdims=True) + 1e-06)


def kernel(n_blk, mean, ls_hbm, bi_hbm, img_hbm, txt_hbm, loss_hbm, gi_hbm, gt_hbm,
           ls_ref, bi_ref, img, txt, gi, gt, row, kept, ib, tb, coef, loss, sib_out, sib_in,
           t_out, t_mid, t_in, i_out, i_mid, i_in, l_mid, l_in, lsem, ssem, rsem):
    rows, width = img.shape
    half = rows // 2
    h0, h1 = pl.ds(0, half), pl.ds(half, half)
    quarters = [pl.ds(at, half // 2) for at in range(0, rows, half // 2)]
    blk = lax.axis_index("blk")
    sibling, pair, near_to, near_of, right, left = places(n_blk)
    barrier = pltpu.get_barrier_semaphore()
    others = [sibling, pair, near_of, right, left]
    for other in others:
        pl.semaphore_signal(barrier, inc=1, device_id=other, device_id_type=MESH)

    load_t = pltpu.make_async_copy(txt_hbm, txt, lsem.at[0])
    load_i = pltpu.make_async_copy(img_hbm, img, lsem.at[1])
    load_t.start()
    load_i.start()
    load_s = pltpu.make_async_copy(ls_hbm, ls_ref, lsem.at[2])
    load_b = pltpu.make_async_copy(bi_hbm, bi_ref, lsem.at[3])
    load_s.start()
    load_b.start()

    sent, landed = [], []

    def copy_to(src, dst, to, with_=None):
        if with_ is None:
            landed.append(None)
        slot = len(landed) - 1 if with_ is None else with_[1]
        copy = pltpu.make_async_remote_copy(
            src_ref=src, dst_ref=dst, send_sem=ssem.at[0], recv_sem=rsem.at[slot],
            device_id=to, device_id_type=MESH)
        sent.append(copy)
        return copy, slot

    def start(*copies):
        for c, _ in copies:
            c.start()

    def arrived(name, *copies):
        with jax.named_scope("wait_" + name):
            for c, _ in copies:
                c.wait_recv()

    def all_arrived(name, into, copy):
        with jax.named_scope("wait_" + name):
            pltpu.make_async_copy(into, into, rsem.at[copy[1]]).wait()

    with jax.named_scope("normalize_text"):
        load_t.wait()
        inv_t = inverse_norm(txt[...])
        tb[OWN0] = (txt[...] * inv_t).astype(BF)
    with jax.named_scope("barrier"):
        pl.semaphore_wait(barrier, len(others))

    t_p0 = copy_to(tb.at[OWN0, h0], tb.at[PAIR0, h0], pair)
    t_n = [copy_to(tb.at[OWN0, q], tb.at[NEAR0, q], near_to) for q in quarters]
    t_p1 = copy_to(tb.at[OWN0, h1], tb.at[PAIR0, h1], pair)
    s_own = copy_to(tb.at[OWN0], tb.at[OWN1], sibling)
    start(t_n[3], t_p0, t_n[2], t_p1, t_n[1], t_n[0], s_own)
    with jax.named_scope("normalize_image"):
        load_i.wait()
        inv_i = inverse_norm(img[...])
        ib[0] = (img[...] * inv_i).astype(BF)
    i_r0 = copy_to(ib.at[0, h0], ib.at[LEFT, h0], right)
    i_l1 = copy_to(ib.at[0, h1], ib.at[RIGHT, h1], left)
    i_r1 = copy_to(ib.at[0, h1], ib.at[LEFT, h1], right)
    i_l0 = copy_to(ib.at[0, h0], ib.at[RIGHT, h0], left)
    start(i_r0, i_l1, i_r1, i_l0)
    i_o0 = copy_to(ib.at[LEFT, h0], ib.at[OPP, h0], right)
    i_o1 = copy_to(ib.at[RIGHT, h1], ib.at[OPP, h1], left, i_o0)
    s_p0 = copy_to(tb.at[PAIR0, h0], tb.at[PAIR1, h0], sibling, s_own)
    s_n1 = copy_to(tb.at[NEAR0, h1], tb.at[NEAR1, h1], sibling)
    s_p1 = copy_to(tb.at[PAIR0, h1], tb.at[PAIR1, h1], sibling, s_own)
    s_n0 = copy_to(tb.at[NEAR0, h0], tb.at[NEAR1, h0], sibling, s_n1)
    s_f0 = copy_to(tb.at[FAR0, h0], tb.at[FAR1, h0], sibling)
    s_f1 = copy_to(tb.at[FAR0, h1], tb.at[FAR1, h1], sibling, s_f0)
    t_f0 = copy_to(tb.at[PAIR0, h0], tb.at[FAR0, h0], near_to)
    t_f1 = copy_to(tb.at[NEAR0, h1], tb.at[FAR0, h1], pair)
    t_q = [copy_to(tb.at[PAIR0, quarters[0]], tb.at[FAR0, quarters[0]], near_to, t_f0),
           copy_to(tb.at[NEAR0, quarters[1]], tb.at[FAR0, quarters[1]], pair),
           copy_to(tb.at[NEAR0, quarters[2]], tb.at[FAR0, quarters[2]], pair),
           copy_to(tb.at[NEAR0, quarters[3]], tb.at[FAR0, quarters[3]], pair, t_f1)]
    into_first = blk == n_blk - 1
    first = blk == 0

    load_s.wait()
    load_b.wait()
    temper = jnp.exp(jnp.full((1, 1), ls_ref[0], F32))
    offset = bi_ref[0]
    loss[...] = jnp.zeros_like(loss)

    def score(first, last, lo, hi):
        with jax.named_scope(f"score_{first}_{last}_{lo}_{hi}"):
            n, m = (last - first) * rows, (hi - lo) * rows
            dots = lax.dot_general(tb[first:last].reshape(n, width), ib[lo:hi].reshape(m, width),
                                   (((1,), (1,)), ((), ())), preferred_element_type=F32)
            logit = temper * dots + offset
            e = jnp.exp(-jnp.abs(logit))
            signed, paired = logit, None
            if first == OWN0 and lo == 0:
                r = lax.broadcasted_iota(jnp.int32, logit.shape, 0)
                paired = (r == lax.broadcasted_iota(jnp.int32, logit.shape, 1)) & (r < rows)
                signed = jnp.where(paired, -logit, logit)
            weight = jnp.where(signed >= 0, 1.0, e) * pl.reciprocal(1.0 + e, approx=True)
            if paired is not None:
                weight = jnp.where(paired, -weight, weight)
            coef[pl.ds(first * rows, n), pl.ds(lo * rows, m)] = (temper * weight).astype(BF)
            e = e.reshape(n // (8 * GROUP), GROUP, 8, m)
            p = e[:, 0]
            for g in range(1, GROUP):
                p = p + e[:, g] * (1.0 + p)
            log1p = jnp.where(p < 1e-3, p * (1.0 - 0.5 * p), jnp.log(1.0 + p))
            lost = (jnp.sum(jnp.maximum(signed, 0.0).reshape(n // 8, 8, m), axis=0)
                    + jnp.sum(log1p, axis=0))
            for slot in range(lo, hi):
                loss[slot] += lost[:, (slot - lo) * rows:(slot - lo + 1) * rows]

    def image_partial(lo, hi, first, last):
        return lax.dot_general(coef[first * rows:last * rows, lo * rows:hi * rows],
                               tb[first:last].reshape((last - first) * rows, width),
                               (((0,), (0,)), ((), ())), preferred_element_type=F32)

    back = [copy_to(sib_out.at[s], sib_in.at[s], sibling) for s in range(4)]
    f_p0 = copy_to(t_out.at[FAR - 1, h0], t_mid.at[0], pair)
    f_n1 = copy_to(t_out.at[FAR - 1, h1], t_mid.at[1], near_of)
    b_p0 = copy_to(t_out.at[PAIR - 1, h0], t_in.at[0, h0], pair)
    b_p1 = copy_to(t_out.at[PAIR - 1, h1], t_in.at[0, h1], pair, b_p0)
    b_n1 = copy_to(t_out.at[NEAR - 1, h1], t_in.at[1, h1], near_of, b_p0)
    b_n0 = copy_to(t_out.at[NEAR - 1, h0], t_in.at[1, h0], near_of, b_p0)
    f_r0 = copy_to(i_out.at[OPP - 1, h0], i_mid.at[0], right)
    f_l1 = copy_to(i_out.at[OPP - 1, h1], i_mid.at[1], left)
    b_r1 = copy_to(i_out.at[RIGHT - 1, h1], i_in.at[0, h1], right)
    b_r0 = copy_to(i_out.at[RIGHT - 1, h0], i_in.at[0, h0], right, b_r1)
    b_l0 = copy_to(i_out.at[LEFT - 1, h0], i_in.at[1, h0], left, b_r1)
    b_l1 = copy_to(i_out.at[LEFT - 1, h1], i_in.at[1, h1], left, b_r1)
    l_o = copy_to(loss.at[OPP], l_mid, right)
    l_r = copy_to(loss.at[RIGHT], l_in.at[0], right)
    l_l = copy_to(loss.at[LEFT], l_in.at[1], left, l_r)

    def text_partial(first, last):
        return jnp.dot(coef[first * rows:last * rows], ib[...].reshape(4 * rows, width),
                       preferred_element_type=F32)

    def to_sibling(s, part):
        sib_out[s] = part.astype(BF)
        start(back[s])

    def add_sibling(s, part):
        arrived(f"text_sibling_{s}", back[s])
        return part + sib_in[s].astype(F32)

    def pass_on(name, got, src, slot, part, middle, out):
        arrived(name, got)
        src[slot, part] = (src[slot, part].astype(F32) + middle[...].astype(F32)).astype(BF)
        start(out)

    def pass_loss():
        arrived("mid_loss", l_o)
        loss[RIGHT] += l_mid[...]
        start(l_r)

    def pass_right():
        pass_on("mid_r", f_r0, i_out, RIGHT - 1, h0, i_mid.at[0], b_r0)

    def pass_left():
        pass_on("mid_l", f_l1, i_out, LEFT - 1, h1, i_mid.at[1], b_l1)

    def pass_near():
        pass_on("mid_n", f_p0, t_out, NEAR - 1, h0, t_mid.at[0], b_n0)

    def pass_pair():
        pass_on("mid_p", f_n1, t_out, PAIR - 1, h1, t_mid.at[1], b_p1)

    assert len(landed) == N_LANDED
    puts = [pltpu.make_async_copy(held, out, lsem.at[i])
            for i, (held, out) in enumerate(((row, loss_hbm), (gt, gt_hbm), (gi.at[h0], gi_hbm.at[h0]),
                                             (gi.at[h1], gi_hbm.at[h1])))]

    def backnorm(values, inverse, grad):
        unit = values * inverse
        return inverse * (grad - unit * jnp.sum(unit * grad, axis=1, keepdims=True))

    def finish_loss():
        all_arrived("loss", l_in, l_r)
        total = loss[0] + l_in[0] + l_in[1]
        row[...] = jnp.sum(total, axis=0, keepdims=True) / mean
        puts[0].start()

    def finish_image():
        all_arrived("image_back", i_in, b_r1)
        with jax.named_scope("image_norm"):
            for at, put in ((0, puts[2]), (half, puts[3])):
                part = pl.ds(at, half)
                grad = gi[part] + i_in[0, part].astype(F32) + i_in[1, part].astype(F32)
                gi[part] = backnorm(img[part], inv_i[at:at + half], grad)
                put.start()

    def finish_text():
        all_arrived("text_back", t_in, b_p0)
        with jax.named_scope("text_norm"):
            grad = gt[...] + t_in[0].astype(F32) + t_in[1].astype(F32)
            gt[...] = backnorm(txt[...], inv_t, grad)
            puts[1].start()

    def start_own_plane():
        arrived("first_p", t_p0)
        pl.when(into_first)(t_q[0][0].start)
        pl.when(jnp.logical_not(into_first))(t_f0[0].start)
        start(s_p0)
        arrived("first_i", i_r0, i_l1)
        start(i_o0)
        start(i_o1)

    @pl.when(jnp.logical_not(first))
    def _():
        start_own_plane()
        arrived("first_n", t_n[3], t_n[2])
        start(t_f1)
        start(s_n1)
        arrived("second_p", t_p1)
        start(s_p1)
        arrived("second_n", t_n[1], t_n[0])
        start(s_n0)
        arrived("second_i", i_r1, i_l0)
        score(OWN0, OWN1, 0, OPP)
        all_arrived("pair_sibling", tb.at[OWN1:NEAR0], s_own)
        score(OWN1, NEAR0, 0, OPP)
        all_arrived("near_sibling", tb.at[NEAR1], s_n1)
        score(NEAR0, FAR0, 0, OPP)
        arrived("far_t0", t_f0)
        start(s_f0)
        arrived("far_t1", t_f1)
        start(s_f1)
        all_arrived("opp_i", ib.at[OPP], i_o0)
        score(OWN0, FAR0, OPP, OPP + 1)
        score(FAR0, FAR1, 0, OPP + 1)
        all_arrived("far_sibling", tb.at[FAR1], s_f0)
        score(FAR1, FAR1 + 1, 0, OPP + 1)
        start(l_o)
        start(l_l)
        with jax.named_scope("text_far_1"):
            to_sibling(FAR, text_partial(FAR1, FAR1 + 1))
        with jax.named_scope("image_opp"):
            i_out[OPP - 1] = image_partial(OPP, OPP + 1, OWN0, FAR1 + 1).astype(BF)
            start(f_r0)
            start(f_l1)
        with jax.named_scope("text_far_0"):
            t_out[FAR - 1] = add_sibling(FAR, text_partial(FAR0, FAR1)).astype(BF)
            start(f_p0)
            start(f_n1)
        with jax.named_scope("text_mid"):
            mid = text_partial(OWN1, FAR0)
            to_sibling(PAIR, mid[rows:2 * rows])
            to_sibling(NEAR, mid[3 * rows:])
            to_sibling(OWN, mid[:rows])
            near = mid[2 * rows:3 * rows]
        with jax.named_scope("image_next"):
            part = image_partial(RIGHT, LEFT + 1, OWN0, FAR1 + 1)
            i_out[RIGHT - 1:LEFT] = part.astype(BF).reshape(2, rows, width)
            start(b_r1)
            start(b_l0)
        with jax.named_scope("text_near"):
            t_out[NEAR - 1] = add_sibling(NEAR, near).astype(BF)
            start(b_n1)
        with jax.named_scope("text_own"):
            own = text_partial(OWN0, OWN1)
            t_out[PAIR - 1] = add_sibling(PAIR, own[rows:]).astype(BF)
            start(b_p0)
            gt[...] = own[:rows]
        with jax.named_scope("image_own"):
            gi[...] = image_partial(0, 1, OWN0, FAR1 + 1)
        pass_loss()
        pass_right()
        pass_left()
        pass_near()
        pass_pair()
        gt[...] = add_sibling(OWN, gt[...])
        finish_loss()
        finish_image()
        finish_text()

    @pl.when(first)
    def _():
        start_own_plane()
        arrived("second_p", t_p1)
        start(s_p1)
        arrived("second_i", i_r1, i_l0)
        score(OWN0, OWN1, 0, OPP)
        all_arrived("pair_sibling", tb.at[OWN1:NEAR0], s_own)
        score(OWN1, NEAR0, 0, OPP)
        all_arrived("opp_i", ib.at[OPP], i_o0)
        score(OWN0, NEAR0, OPP, OPP + 1)
        arrived("first_n", t_n[3])
        start(t_q[3])
        arrived("second_n", t_n[2])
        start(t_q[2], s_n1)
        with jax.named_scope("text_block"):
            part = text_partial(OWN0, NEAR0)
            to_sibling(PAIR, part[3 * rows:])
            to_sibling(OWN, part[2 * rows:3 * rows])
            gt[...] = part[:rows]
            kept[...] = part[rows:2 * rows]
        arrived("third_n", t_n[1])
        start(t_q[1])
        arrived("last_n", t_n[0])
        start(s_n0)
        score(NEAR0, NEAR1, 0, OPP + 1)
        all_arrived("near_sibling", tb.at[NEAR1], s_n1)
        score(NEAR1, FAR0, 0, OPP + 1)
        arrived("far_t1", t_q[3], t_q[2])
        start(s_f1)
        arrived("far_t0", t_q[0], t_q[1])
        start(s_f0)
        score(FAR0, FAR1, 0, OPP + 1)
        with jax.named_scope("image_ahead"):
            gi[...] = image_partial(OPP, OPP + 1, OWN0, FAR0)
        all_arrived("far_sibling", tb.at[FAR1], s_f0)
        score(FAR1, FAR1 + 1, OPP, OPP + 1)
        with jax.named_scope("image_opp"):
            i_out[OPP - 1] = (gi[...] + image_partial(OPP, OPP + 1, FAR0, FAR1 + 1)).astype(BF)
            start(f_r0, f_l1)
        t_out[PAIR - 1] = add_sibling(PAIR, kept[...]).astype(BF)
        start(b_p0)
        score(FAR1, FAR1 + 1, 0, OPP)
        start(l_o, l_l)
        with jax.named_scope("text_far_1"):
            to_sibling(FAR, text_partial(FAR1, FAR1 + 1))
        with jax.named_scope("image_next"):
            part = image_partial(RIGHT, OPP, OWN0, FAR1 + 1)
            i_out[RIGHT - 1:LEFT] = part.astype(BF).reshape(2, rows, width)
            start(b_r1, b_l0)
        with jax.named_scope("text_far_0"):
            t_out[FAR - 1] = add_sibling(FAR, text_partial(FAR0, FAR1)).astype(BF)
            start(f_p0, f_n1)
        with jax.named_scope("text_near"):
            near = text_partial(NEAR0, FAR0)
            to_sibling(NEAR, near[rows:])
        pass_pair()
        gt[...] = add_sibling(OWN, gt[...])
        t_out[NEAR - 1] = add_sibling(NEAR, near[:rows]).astype(BF)
        start(b_n1)
        with jax.named_scope("image_own"):
            gi[...] = image_partial(0, 1, OWN0, FAR1 + 1)
        pass_loss()
        pass_right()
        pass_left()
        pass_near()
        finish_loss()
        finish_text()
        finish_image()

    with jax.named_scope("sends_end"):
        some = [t_f0[0], t_f1[0]] + [c for c, _ in t_q]
        for c in sent:
            if not any(c is o for o in some):
                c.wait_send()
        pl.when(into_first)(t_q[0][0].wait_send)
        pl.when(jnp.logical_not(into_first))(t_f0[0].wait_send)
        pl.when(jnp.logical_not(first))(t_f1[0].wait_send)
        for c, _ in t_q[1:]:
            pl.when(first)(c.wait_send)
    with jax.named_scope("put"):
        for c in puts:
            c.wait()


def hand_on(row, gi, gt, row_out, gi_out, gt_out, row_held, gi_held, gt_held, in_sem, out_sem):
    parts = [(row, row_held, row_out)]
    size = gi.shape[0] // PARTS
    for at in range(0, gi.shape[0], size):
        for src, held, out in ((gi, gi_held, gi_out), (gt, gt_held, gt_out)):
            parts.append(tuple(ref.at[pl.ds(at, size)] for ref in (src, held, out)))
    reads = [pltpu.make_async_copy(src, held, in_sem.at[i]) for i, (src, held, _) in enumerate(parts)]
    writes = [pltpu.make_async_copy(held, out, out_sem.at[i]) for i, (_, held, out) in enumerate(parts)]
    for c in reads:
        c.start()
    for r, w in zip(reads, writes):
        r.wait()
        w.start()
    for c in writes:
        c.wait()


def body(images, texts, log_scale, bias):
    rows, width = images.shape
    n_blk = lax.axis_size("blk")
    mean = STEPS * rows * lax.axis_size("grp")
    low = functools.partial(pltpu.VMEM, dtype=BF)
    full = functools.partial(pltpu.VMEM, dtype=F32)
    anywhere = pl.BlockSpec(memory_space=pl.ANY)
    results = (
        jax.ShapeDtypeStruct((1, rows), F32),
        jax.ShapeDtypeStruct((rows, width), F32),
        jax.ShapeDtypeStruct((rows, width), F32),
    )
    held = pl.pallas_call(
        functools.partial(kernel, n_blk, mean),
        out_shape=results,
        in_specs=[anywhere] * 4,
        out_specs=(anywhere,) * 3,
        scratch_shapes=[
            pltpu.SMEM((1,), F32), pltpu.SMEM((1,), F32),
            full((rows, width)), full((rows, width)),
            full((rows, width)), full((rows, width)), full((1, rows)),
            full((rows, width)),
            low((4, rows, width)),
            low((8, rows, width)),
            low((8 * rows, 4 * rows)),
            full((4, 8, rows)),
            low((4, rows, width)), low((4, rows, width)),
            low((3, rows, width)), low((2, rows // 2, width)), low((2, rows, width)),
            low((3, rows, width)), low((2, rows // 2, width)), low((2, rows, width)),
            full((8, rows)), full((2, 8, rows)),
            pltpu.SemaphoreType.DMA((4,)),
            pltpu.SemaphoreType.DMA((1,)),
            pltpu.SemaphoreType.DMA((N_LANDED,)),
        ],
        compiler_params=pltpu.CompilerParams(
            collective_id=0, has_side_effects=True, vmem_limit_bytes=(64 << 20) - (1 << 19)),
        name="pair_loss",
    )(log_scale, bias, images, texts)
    row_loss, image_grad, text_grad = pl.pallas_call(
        hand_on,
        out_shape=results,
        in_specs=[anywhere] * 3,
        out_specs=(anywhere,) * 3,
        scratch_shapes=[
            full((1, rows)), full((rows, width)), full((rows, width)),
            pltpu.SemaphoreType.DMA((2 * PARTS + 1,)), pltpu.SemaphoreType.DMA((2 * PARTS + 1,)),
        ],
        name="hand_on",
    )(*held)
    return row_loss.reshape(rows), image_grad, text_grad


def solution(mesh):
    in_specs = (P(("blk", "grp"), None), P(("blk", "grp"), None), P(), P())
    out_specs = (P(("blk", "grp")), P(("blk", "grp"), None), P(("blk", "grp"), None))
    return jax.shard_map(body, mesh=mesh, in_specs=in_specs, out_specs=out_specs, check_vma=False)
```
